256 devices in a mesh: gx: 16 (over y, x_lo, core), gy: 16 (over z, x_hi).
Axes of the slice: x: 4 (x_hi: 2, x_lo: 2; x = x_hi * 2 + x_lo), y: 4, z: 8, core: 2. Of those that a mesh axis runs over, the one named last changes fastest.
Arguments:
- features: bfloat16 [65536, 128], P(('gx', 'gy')), may hold values from -6 to 6
- w_sub: bfloat16 [27, 128, 128], replicated, may hold values from -0.1875 to 0.1875
- w_down: bfloat16 [1024, 256], replicated, may hold values from -0.25 to 0.25
- cell_ids: int32 [65536], P(('gx', 'gy')), may hold values from -1 to 511, as said below
- send_rows: int32 [73728], P(('gx', 'gy')), may hold values from 0 to 256, as said below
- map_in: int32 [27, 65536], P(None, ('gx', 'gy')), may hold values from 0 to 608, as said below
- map_out: int32 [27, 65536], P(None, ('gx', 'gy')), may hold values from 0 to 256, as said below
- cotangent: bfloat16 [16384, 256], P(('gx', 'gy')), may hold values from -6 to 6
Outputs:
- coarse: bfloat16 [16384, 256], P(('gx', 'gy'))
- feature_grad: bfloat16 [65536, 128], P(('gx', 'gy'))
- sub_grad: float32 [27, 128, 128], replicated
- down_grad: float32 [1024, 256], replicated
The draws below stay inside these ranges and needn't reach their ends.
Inputs may be any that keep to these rules, and one draw needn't show every extreme that they name: `cell_ids`: in every region the used rows are 0 to count - 1, in increasing cell number; -1 marks unused rows; a region uses at most 256 rows and some region uses exactly 256. `send_rows`: the row of the voxel at each rim cell, 256 where the cell is empty; rim cells listed in increasing cell number. `map_in`: indices into lookup_table: below 256 own rows, 257 + g ghost row g; within each offset the pairs come in increasing output row, and unused entries stand at the end with the value 256. A pair exists exactly where the output voxel and the voxel at its offset both exist. `map_out`: the output row of each pair; 256 on unused entries at the end of each offset's list; each row appears at most once per offset.
All inputs are finite; a program needn't handle non-finite values.
Results may differ from the reference program's by a relative error of at most 0.015.
Values may be sent and summed in bfloat16 or wider, within the bound.
No kernel may reach another device: no remote copies, remote signals or barrier semaphores. Data moves between devices by JAX's collectives and lax.ppermute only.
A program may use at most 64 MiB of HBM per device.

```python
import jax
import jax.numpy as jnp
import numpy as np
from jax import lax

C = 128
C2 = 256
OFFSETS = 27
LX = 4
LY = 16
LZ = 8
V_DEV = 256
U_DEV = 64
FACE = 288
GHOST = 352
VOXELS = 65536
COARSE = 16384
N_GX = 16
N_GY = 16


def frame_starts():
    start_table = np.zeros((LX + 2, LY + 2), np.int64)
    counter = 0
    for frame_x in range(-1, LX + 1):
        for frame_y in range(-1, LY + 1):
            if 0 <= frame_x < LX and 0 <= frame_y < LY:
                continue
            start_table[frame_x + 1, frame_y + 1] = counter
            counter += LZ
    return start_table


def geometry(key):
    cell_count = LX * LY * LZ
    regions = N_GX * N_GY
    key_base, key_hot, key_full, key_shuffle = jax.random.split(key, 4)
    base_count = jax.random.randint(key_base, (regions,), V_DEV // 4, V_DEV // 2 + 1)
    hot_region = jax.random.randint(key_hot, (regions,), 0, 8) == 0
    full_region = jax.random.randint(key_full, (), 0, regions)
    counts = jnp.where(hot_region | (jnp.arange(regions) == full_region), V_DEV, base_count)
    region_keys = jax.random.split(key_shuffle, regions)
    shuffled = jax.vmap(lambda region_key: jax.random.permutation(region_key, cell_count))(region_keys)
    position = jnp.argsort(shuffled, axis=1)
    active = position < counts[:, None]
    row_of = jnp.where(active, jnp.cumsum(active.astype(jnp.int32), axis=1) - 1, V_DEV).astype(jnp.int32)
    cell_range = jnp.broadcast_to(jnp.arange(cell_count, dtype=jnp.int32), (regions, cell_count))
    region_index = jnp.arange(regions)[:, None]
    cell_table = jnp.full((regions, V_DEV + 1), -1, jnp.int32).at[region_index, row_of].set(cell_range)
    return (active, row_of, cell_table[:, :V_DEV])


def kernel_maps(key):
    active, row_of, cell_table = geometry(key)
    regions = N_GX * N_GY
    cell_index = np.arange(LX * LY * LZ)
    coord_x = cell_index // (LY * LZ)
    coord_y = cell_index // LZ % LY
    coord_z = cell_index % LZ
    region_x = np.arange(regions) // N_GY
    region_y = np.arange(regions) % N_GY
    global_active = active.reshape(N_GX, N_GY, LX, LY, LZ).transpose(0, 2, 1, 3, 4).reshape(N_GX * LX, N_GY * LY, LZ)
    global_active = jnp.pad(global_active, 1)
    start_table = frame_starts()
    gather_in, gather_out = ([], [])
    for step_x in (-1, 0, 1):
        for step_y in (-1, 0, 1):
            for step_z in (-1, 0, 1):
                near_x = coord_x + step_x
                near_y = coord_y + step_y
                near_z = coord_z + step_z
                global_x = region_x[:, None] * LX + near_x[None, :] + 1
                global_y = region_y[:, None] * LY + near_y[None, :] + 1
                is_valid = active & global_active[global_x, global_y, (near_z + 1)[None, :]]
                inside = (near_x >= 0) & (near_x < LX) & (near_y >= 0) & (near_y < LY)
                clip_z = np.clip(near_z, 0, LZ - 1)
                own_cell = (np.clip(near_x, 0, LX - 1) * LY + np.clip(near_y, 0, LY - 1)) * LZ + clip_z
                ghost_index = V_DEV + 1 + start_table[near_x + 1, near_y + 1] + clip_z
                source = jnp.where(inside[None, :], row_of[:, own_cell], jnp.asarray(ghost_index, jnp.int32)[None, :])
                ordering = jnp.argsort(jnp.where(is_valid, 0, 1), axis=1, stable=True)[:, :V_DEV]
                gather_in.append(jnp.take_along_axis(jnp.where(is_valid, source, V_DEV), ordering, axis=1))
                gather_out.append(jnp.take_along_axis(jnp.where(is_valid, row_of, V_DEV), ordering, axis=1))
    map_in = jnp.stack(gather_in).reshape(OFFSETS, regions * V_DEV).astype(jnp.int32)
    map_out = jnp.stack(gather_out).reshape(OFFSETS, regions * V_DEV).astype(jnp.int32)
    return (map_in, map_out)


def draw_cell_ids(key, part):
    return geometry(key)[2].reshape(-1)


def draw_send_rows(key, part):
    active, row_of, cell_table = geometry(key)
    cell_index = np.arange(LX * LY * LZ)
    coord_x = cell_index // (LY * LZ)
    coord_y = cell_index // LZ % LY
    on_rim = (coord_x == 0) | (coord_x == LX - 1) | (coord_y == 0) | (coord_y == LY - 1)
    return row_of[:, cell_index[on_rim]].reshape(-1).astype(jnp.int32)


def draw_map_in(key, part):
    return kernel_maps(key)[0]


def draw_map_out(key, part):
    return kernel_maps(key)[1]


def level_of(key, dims, cuts, low, high):
    loudness = 1.0
    for dim, shards_of in cuts:
        draws = jax.random.uniform(jax.random.fold_in(jax.random.fold_in(key, 6), dim), (shards_of,), jnp.float32, low / len(cuts), high / len(cuts))
        loudness = loudness * jnp.repeat(jnp.exp(draws), dims[dim] // shards_of).reshape((-1,) + (1,) * (len(dims) - 1 - dim))
    return loudness


def noise(own_key, shape, scale, bound, cuts=(), held_as=jnp.bfloat16):
    array = scale * jax.random.normal(own_key, shape, jnp.float32)
    if cuts:
        array = array * level_of(own_key, shape, cuts, -0.22, 0.18)
    return jnp.clip(array, -bound, bound).astype(held_as)


def setup_inputs(seed: int = 0) -> dict:
    seeds = jax.random.split(jax.random.key(seed), 9)
    features = noise(seeds[0], (VOXELS, C), 1.0, 6.0, ((0, 256),))
    w_sub = noise(seeds[1], (OFFSETS, C, C), (9 * C) ** -0.5, 0.1875)
    w_down = noise(seeds[2], (8 * C, C2), (4 * C) ** -0.5, 0.25)
    cell_ids = draw_cell_ids(jax.random.fold_in(seeds[8], 71), 0)
    send_rows = draw_send_rows(jax.random.fold_in(seeds[8], 71), 0)
    map_in = draw_map_in(jax.random.fold_in(seeds[8], 71), 0)
    map_out = draw_map_out(jax.random.fold_in(seeds[8], 71), 0)
    cotangent = noise(seeds[7], (COARSE, C2), 1.0, 6.0, ((0, 256),))
    return {"features": features, "w_sub": w_sub, "w_down": w_down, "cell_ids": cell_ids, "send_rows": send_rows, "map_in": map_in, "map_out": map_out, "cotangent": cotangent}


def frame_tables():
    cell_count = LX * LY * LZ
    cell_index = np.arange(cell_count)
    coord_x = cell_index // (LY * LZ)
    coord_y = cell_index // LZ % LY
    on_rim = (coord_x == 0) | (coord_x == LX - 1) | (coord_y == 0) | (coord_y == LY - 1)
    rim_place = np.full(cell_count, -1, np.int64)
    rim_place[on_rim] = np.arange(int(on_rim.sum()))
    depth_range = np.arange(LZ)
    neighbour_list, face_list, side_list = ([], [], [])
    for frame_x in range(-1, LX + 1):
        for frame_y in range(-1, LY + 1):
            if 0 <= frame_x < LX and 0 <= frame_y < LY:
                continue
            step_x = -1 if frame_x < 0 else 1 if frame_x >= LX else 0
            step_y = -1 if frame_y < 0 else 1 if frame_y >= LY else 0
            local_cell = ((frame_x - step_x * LX) * LY + (frame_y - step_y * LY)) * LZ + depth_range
            neighbour_list.append(np.full(LZ, (step_x + 1) * 3 + step_y + 1))
            face_list.append(rim_place[local_cell])
            if 0 <= frame_y < LY:
                first_place = (0 if frame_x < 0 else LY * LZ) + frame_y * LZ
            else:
                column = frame_x if 0 <= frame_x < LX else LX if frame_x < 0 else LX + 1
                first_place = 2 * LY * LZ + (0 if frame_y < 0 else (LX + 2) * LZ) + column * LZ
            side_list.append(first_place + depth_range)
    side_place = np.concatenate(side_list)

    def face_rows(spots):
        return np.concatenate([rim_place[(spot_x * LY + spot_y) * LZ + depth_range] for spot_x, spot_y in spots])
    return {'neighbour': np.concatenate(neighbour_list), 'face': np.concatenate(face_list), 'side_place': side_place, 'side_order': np.argsort(side_place), 'x_high': face_rows([(LX - 1, column_y) for column_y in range(LY)]), 'x_low': face_rows([(0, column_y) for column_y in range(LY)]), 'y_high': face_rows([(column_x, LY - 1) for column_x in range(LX)]), 'y_low': face_rows([(column_x, 0) for column_x in range(LX)])}

def coarse_slot(cell_ids):
    coord_x = cell_ids // (LY * LZ)
    coord_y = cell_ids // LZ % LY
    coord_z = cell_ids % LZ
    coarse_cell = (coord_x // 2 * (LY // 2) + coord_y // 2) * (LZ // 2) + coord_z // 2
    corner = coord_x % 2 * 4 + coord_y % 2 * 2 + coord_z % 2
    return jnp.where(cell_ids >= 0, coarse_cell * 8 + corner, U_DEV * 8).astype(jnp.int32)

def take_rows(values, picks):
    return jax.vmap(lambda block, chosen: block[chosen])(values, picks)

def reference(features, w_sub, w_down, cell_ids, send_rows, map_in, map_out, cotangent):
    frames = frame_tables()
    regions = N_GX * N_GY
    region_features = features.reshape(regions, V_DEV, C)
    region_send = send_rows.reshape(regions, FACE)
    taps_in = map_in.reshape(OFFSETS, regions, V_DEV)
    taps_out = map_out.reshape(OFFSETS, regions, V_DEV)
    slot_index = coarse_slot(cell_ids.reshape(regions, V_DEV))

    def ghost_of(values):
        padded = jnp.concatenate([values, jnp.zeros((regions, 1, C), values.dtype)], 1)
        rim_rows = take_rows(padded, region_send)
        grid_rows = jnp.pad(rim_rows.reshape(N_GX, N_GY, FACE, C), ((1, 1), (1, 1), (0, 0), (0, 0)))
        windows = jnp.stack([grid_rows[row_step:row_step + N_GX, col_step:col_step + N_GY] for row_step in range(3) for col_step in range(3)])
        picked = windows[frames['neighbour'], :, :, frames['face']]
        return picked.transpose(1, 2, 0, 3).reshape(regions, GHOST, C)
    ghost_rows = ghost_of(region_features.astype(jnp.float32)).astype(jnp.bfloat16)
    lookup_table = jnp.concatenate([region_features, jnp.zeros((regions, 1, C), jnp.bfloat16), ghost_rows], 1)

    def forward_step(accumulated, scan_item):
        source, target, weight = scan_item
        gathered = take_rows(lookup_table, source)
        product = jnp.dot(gathered.reshape(-1, C), weight, preferred_element_type=jnp.float32).reshape(regions, V_DEV, C)
        accumulated = jax.vmap(lambda total, where_to, terms: total.at[where_to].add(terms))(accumulated, target, product)
        return (accumulated, None)
    summed, _ = lax.scan(forward_step, jnp.zeros((regions, V_DEV + 1, C), jnp.float32), (taps_in, taps_out, w_sub))
    pre_act = summed[:, :V_DEV]
    hidden = jax.nn.silu(pre_act).astype(jnp.bfloat16)
    coarse_input = jax.vmap(lambda chosen, rows_in: jnp.zeros((U_DEV * 8 + 1, C), jnp.bfloat16).at[chosen].set(rows_in)[:U_DEV * 8])(slot_index, hidden)
    coarse_input = coarse_input.reshape(regions * U_DEV, 8 * C)
    coarse = jnp.dot(coarse_input, w_down, preferred_element_type=jnp.float32).astype(jnp.bfloat16)
    back_rows = jnp.dot(cotangent, w_down.T, preferred_element_type=jnp.float32).astype(jnp.bfloat16)
    back_rows = jnp.concatenate([back_rows.reshape(regions, U_DEV * 8, C), jnp.zeros((regions, 1, C), jnp.bfloat16)], 1)
    hidden_grad = take_rows(back_rows, slot_index)
    sigmoid_value = jax.nn.sigmoid(pre_act)
    pre_grad = (hidden_grad.astype(jnp.float32) * sigmoid_value * (1.0 + pre_act * (1.0 - sigmoid_value))).astype(jnp.bfloat16)
    down_grad = jnp.dot(coarse_input.T, cotangent, preferred_element_type=jnp.float32)
    grad_ext = jnp.concatenate([pre_grad, jnp.zeros((regions, 1, C), jnp.bfloat16)], 1)

    def backward_step(accumulated, scan_item):
        source, target, weight = scan_item
        gathered = take_rows(lookup_table, source).reshape(-1, C)
        grad_rows = take_rows(grad_ext, target).reshape(-1, C)
        weight_grad = jnp.dot(gathered.T, grad_rows, preferred_element_type=jnp.float32)
        spread = jnp.dot(grad_rows, weight.T, preferred_element_type=jnp.float32).reshape(regions, V_DEV, C)
        accumulated = jax.vmap(lambda total, where_to, terms: total.at[where_to].add(terms))(accumulated, source, spread)
        return (accumulated, weight_grad)
    table_grad, sub_grad = lax.scan(backward_step, jnp.zeros((regions, V_DEV + 1 + GHOST, C), jnp.float32), (taps_in, taps_out, w_sub))
    _, pull_back = jax.vjp(ghost_of, region_features.astype(jnp.float32))
    from_ghost = pull_back(table_grad[:, V_DEV + 1:])[0]
    feature_grad = (table_grad[:, :V_DEV] + from_ghost).astype(jnp.bfloat16).reshape(VOXELS, C)
    return (coarse, feature_grad, sub_grad, down_grad)
```

```python
import jax
import jax.numpy as jnp
from jax import lax
from jax.experimental import pallas as pl
from jax.experimental.pallas import tpu as pltpu
from jax.sharding import PartitionSpec as P

LX = 4
LY = 16
LZ = 8
CELLS = LX * LY * LZ
U_DEV = 64
C = 128
C2 = 256
OFFSETS = 27
AXES = ("gx", "gy")
PEERS = 128
CHUNK = 24
HALF = PEERS * CHUNK
HALF_BLOCKS = HALF // C

F32 = jnp.float32
BF16 = jnp.bfloat16


def swap_pairs(count):
    even = [(k, k ^ 1) for k in range(count)]
    odd = [(k, k + 1 if k % 2 else k - 1) for k in range(count)]
    return even, [(k, m) for k, m in odd if 0 <= m < count]


def swap_both(first, second, axis):
    even, odd = swap_pairs(lax.axis_size(axis))
    return lax.ppermute(first, axis, even), lax.ppermute(second, axis, odd)


def parity(axis):
    return lax.rem(lax.axis_index(axis), 2)


def pick(flag, when_zero, when_one):
    mask = jnp.full(when_zero.shape, flag, jnp.int32) == 0
    return jnp.where(mask, when_zero, when_one)


def dot(left, right, dims=((1,), (0,))):
    return lax.dot_general(left, right, (dims, ((), ())), preferred_element_type=F32)


def cell_onehot(ids):
    cells = lax.broadcasted_iota(jnp.int32, (CELLS, ids.shape[1]), 0)
    return jnp.where(cells == ids, 1.0, 0.0).astype(BF16)


def corner_onehot(row_axis):
    place = lax.broadcasted_iota(jnp.int32, (CELLS, CELLS), row_axis)
    cell = lax.broadcasted_iota(jnp.int32, (CELLS, CELLS), 1 - row_axis)
    corner, row = place >> 6, place & 63
    x = ((row >> 5) << 1) + (corner >> 2)
    y = (((row >> 2) & 7) << 1) + ((corner >> 1) & 1)
    z = ((row & 3) << 1) + (corner & 1)
    return jnp.where(((x * LY + y) * LZ + z) == cell, 1.0, 0.0).astype(BF16)


def shift_z(value, step):
    rows = value.shape[0]
    z = lax.broadcasted_iota(jnp.int32, value.shape, 0) & (LZ - 1)
    if step == 1:
        return jnp.where(z == 0, 0.0, pltpu.roll(value, 1, 0))
    return jnp.where(z == LZ - 1, 0.0, pltpu.roll(value, rows - 1, 0))


def store_y_sides(grid, even_ref, odd_ref):
    low = grid[:, 0].reshape(LX * LZ, C)
    high = grid[:, LY - 1].reshape(LX * LZ, C)
    side = parity("gy")
    even_ref[...] = pick(side, high, low).astype(BF16)
    odd_ref[...] = pick(side, low, high).astype(BF16)


def y_halos(even_ref, odd_ref):
    even, odd = even_ref[...].astype(F32), odd_ref[...].astype(F32)
    side = parity("gy")
    low = pick(side, odd, even).reshape(LX, LZ, C)
    high = pick(side, even, odd).reshape(LX, LZ, C)
    return low, high


def build_kernel(ids_ref, features_ref, grid_ref, even_ref, odd_ref):
    dense = dot(cell_onehot(ids_ref[...]), features_ref[...])
    grid_ref[...] = dense.astype(BF16)
    store_y_sides(dense.reshape(LX, LY, LZ, C), even_ref, odd_ref)


def x_sides_kernel(grid_ref, y_even_ref, y_odd_ref, even_ref, odd_ref):
    plane = LY * LZ
    y_low, y_high = y_halos(y_even_ref, y_odd_ref)
    first = jnp.concatenate([y_low[0], grid_ref[:plane].astype(F32), y_high[0]], 0)
    last = jnp.concatenate([y_low[LX - 1], grid_ref[CELLS - plane :].astype(F32), y_high[LX - 1]], 0)
    side = parity("gx")
    even_ref[...] = pick(side, last, first).astype(BF16)
    odd_ref[...] = pick(side, first, last).astype(BF16)


def fill_padded(padded, grid_ref, y_even_ref, y_odd_ref, x_even_ref, x_odd_ref):
    y_low, y_high = y_halos(y_even_ref, y_odd_ref)
    x_even, x_odd = x_even_ref[...].astype(F32), x_odd_ref[...].astype(F32)
    side = parity("gx")
    padded[0] = pick(side, x_odd, x_even).reshape(LY + 2, LZ, C)
    padded[LX + 1] = pick(side, x_even, x_odd).reshape(LY + 2, LZ, C)
    padded[1 : LX + 1, 0] = y_low
    padded[1 : LX + 1, LY + 1] = y_high
    padded[1 : LX + 1, 1 : LY + 1] = grid_ref[...].astype(F32).reshape(LX, LY, LZ, C)


def columns(padded, step_x, step_y):
    window = padded[step_x : step_x + LX, step_y : step_y + LY]
    return window.reshape(CELLS, C).astype(BF16)


def main_kernel(
    ids_ref, grid_ref, y_even_ref, y_odd_ref, x_even_ref, x_odd_ref, w_sub_ref, w_down_ref, cot_ref,
    coarse_ref, grad_ref, grad_even_ref, grad_odd_ref, own_ref, send_ref, padded, sums,
):
    fill_padded(padded, grid_ref, y_even_ref, y_odd_ref, x_even_ref, x_odd_ref)
    parts = [jnp.zeros((CELLS, C), F32)] * 3
    for step_x in range(3):
        for step_y in range(3):
            window = columns(padded, step_x, step_y)
            first = step_x * 9 + step_y * 3
            parts = [parts[k] + dot(window, w_sub_ref[first + k]) for k in range(3)]
    pre_act = shift_z(parts[0], 1) + parts[1] + shift_z(parts[2], -1)
    active = dot(cell_onehot(ids_ref[...]), jnp.ones((ids_ref.shape[1], C), BF16)) > 0.5
    sigmoid = 1.0 / (1.0 + jnp.exp(-pre_act))
    hidden = jnp.where(active, pre_act * sigmoid, 0.0).astype(BF16)
    by_corner = dot(corner_onehot(0), hidden).astype(BF16)
    coarse_input = jnp.concatenate([by_corner[k * U_DEV : (k + 1) * U_DEV] for k in range(8)], 1)
    cot = cot_ref[...]
    w_down = w_down_ref[...]
    coarse_ref[...] = dot(coarse_input, w_down).astype(BF16)
    back_rows = dot(cot, w_down, ((1,), (1,))).astype(BF16)
    stacked = jnp.concatenate([back_rows[:, k * C : (k + 1) * C] for k in range(8)], 0)
    hidden_grad = dot(corner_onehot(1), stacked)
    pre_grad = hidden_grad * sigmoid * (1.0 + pre_act * (1.0 - sigmoid))
    pre_grad = jnp.where(active, pre_grad, 0.0).astype(BF16)
    grad_ref[...] = pre_grad
    grad = pre_grad.astype(F32)
    store_y_sides(grad.reshape(LX, LY, LZ, C), grad_even_ref, grad_odd_ref)
    spread = jnp.concatenate([shift_z(grad, -1), grad, shift_z(grad, 1)], 1).astype(BF16)
    for step_x in range(3):
        for step_y in range(3):
            first = (step_x * 9 + step_y * 3) * C
            taps = dot(columns(padded, step_x, step_y), spread, ((0,), (0,)))
            for k in range(3):
                sums[first + k * C : first + (k + 1) * C] = taps[:, k * C : (k + 1) * C]
    down = dot(coarse_input, cot, ((0,), (0,)))
    base = OFFSETS * C
    sums[base : base + 8 * C] = down[:, :C]
    sums[base + 8 * C : base + 16 * C] = down[:, C:]
    sums[base + 16 * C :] = jnp.zeros((2 * HALF - base - 16 * C, C), F32)
    mine = parity("gx")
    start = pl.multiple_of(mine * HALF, HALF)
    other = pl.multiple_of((1 - mine) * HALF, HALF)
    own_ref[...] = sums[pl.ds(start, HALF)].reshape(PEERS, CHUNK, C).astype(BF16)
    send_ref[...] = sums[pl.ds(other, HALF)].reshape(PEERS, CHUNK, C).astype(BF16)


def feature_kernel(ids_ref, grid_ref, y_even_ref, y_odd_ref, x_even_ref, x_odd_ref, w_sub_ref, out_ref, padded):
    fill_padded(padded, grid_ref, y_even_ref, y_odd_ref, x_even_ref, x_odd_ref)
    parts = [jnp.zeros((CELLS, C), F32)] * 3
    for step_x in range(3):
        for step_y in range(3):
            window = columns(padded, 2 - step_x, 2 - step_y)
            first = step_x * 9 + step_y * 3
            parts = [parts[k] + dot(window, w_sub_ref[first + k], ((1,), (1,))) for k in range(3)]
    total = shift_z(parts[0], -1) + parts[1] + shift_z(parts[2], 1)
    out_ref[...] = dot(cell_onehot(ids_ref[...]), total.astype(BF16), ((0,), (0,))).astype(BF16)


def unpack_kernel(own_ref, other_ref, sub_ref, down_ref, sums):
    mine = parity("gx")
    start = pl.multiple_of(mine * HALF, HALF)
    other = pl.multiple_of((1 - mine) * HALF, HALF)
    sums[pl.ds(start, HALF)] = own_ref[...].astype(F32).reshape(HALF, C)
    sums[pl.ds(other, HALF)] = other_ref[...].astype(F32).reshape(HALF, C)
    base = OFFSETS * C
    sub_ref[...] = sums[:base].reshape(OFFSETS, C, C)
    down_ref[:, :C] = sums[base : base + 8 * C]
    down_ref[:, C:] = sums[base + 8 * C : base + 16 * C]


def call(kernel, outs, scratch=()):
    def shape(dims, dtype):
        return jax.ShapeDtypeStruct(dims, dtype)

    return pl.pallas_call(
        kernel,
        out_shape=[shape(*out) for out in outs],
        scratch_shapes=list(scratch),
        compiler_params=pltpu.CompilerParams(vmem_limit_bytes=40 * 1024 * 1024),
    )


def halo(grid, y_even, y_odd):
    y_even, y_odd = swap_both(y_even, y_odd, "gy")
    rows = (LY + 2) * LZ
    sides = call(x_sides_kernel, [((rows, C), BF16)] * 2)(grid, y_even, y_odd)
    x_even, x_odd = swap_both(*sides, "gx")
    return grid, y_even, y_odd, x_even, x_odd


def core_swap(value):
    return lax.ppermute(value, "gx", swap_pairs(lax.axis_size("gx"))[0])


def reduce_all(own, send):
    rows, cols = lax.axis_size("gx"), lax.axis_size("gy")
    groups = [[i * cols + j for i in range(core, rows, 2) for j in range(cols)] for core in range(2)]

    def trade(value):
        return lax.all_to_all(value, AXES, 0, 0, axis_index_groups=groups, tiled=True)

    part = (own.astype(F32) + core_swap(send).astype(F32)).astype(BF16)
    mine = trade(part).astype(F32).sum(0).astype(BF16)
    whole = trade(jnp.broadcast_to(mine[None], (PEERS, CHUNK, C)))
    return whole, core_swap(whole)


def local(features, w_sub, w_down, cell_ids, send_rows, map_in, map_out, cotangent):
    ids = cell_ids[None]
    side = ((LX * LZ, C), BF16)
    dense = ((CELLS, C), BF16)
    packed = ((PEERS, CHUNK, C), BF16)
    padded = pltpu.VMEM((LX + 2, LY + 2, LZ, C), F32)
    sums = pltpu.VMEM((2 * HALF, C), F32)
    grid, y_even, y_odd = call(build_kernel, [dense, side, side])(ids, features)
    coarse, grad, grad_even, grad_odd, own, send = call(
        main_kernel, [((U_DEV, C2), BF16), dense, side, side, packed, packed], [padded, sums]
    )(ids, *halo(grid, y_even, y_odd), w_sub, w_down, cotangent)
    (feature_grad,) = call(feature_kernel, [((features.shape[0], C), BF16)], [padded])(
        ids, *halo(grad, grad_even, grad_odd), w_sub
    )
    sub_grad, down_grad = call(
        unpack_kernel, [((OFFSETS, C, C), F32), ((8 * C, C2), F32)], [sums]
    )(*reduce_all(own, send))
    return coarse, feature_grad, sub_grad, down_grad


def solution(mesh):
    rows = P(AXES, None)
    flat = P(AXES)
    maps = P(None, AXES)
    return jax.shard_map(
        local,
        mesh=mesh,
        in_specs=(rows, P(), P(), flat, flat, maps, maps, rows),
        out_specs=(rows, rows, P(), P()),
        check_vma=False,
    )
```

```python
import jax
import jax.numpy as jnp
from jax import lax
from jax.experimental import pallas as pl
from jax.experimental.pallas import tpu as pltpu
from jax.sharding import PartitionSpec as P

LX = 4
LY = 16
LZ = 8
CELLS = LX * LY * LZ
U_DEV = 64
C = 128
C2 = 256
OFFSETS = 27
AXES = ("gx", "gy")
CHUNK = 176
HALF = 16 * CHUNK
LONG = 1 << 33

F32 = jnp.float32
BF16 = jnp.bfloat16


def swap_pairs(count):
    even = [(k, k ^ 1) for k in range(count)]
    odd = [(k, k + 1 if k % 2 else k - 1) for k in range(count)]
    return even, [(k, m) for k, m in odd if 0 <= m < count]


def swap_both(first, second, axis):
    even, odd = swap_pairs(lax.axis_size(axis))
    second = lax.ppermute(second, axis, odd)
    return lax.ppermute(first, axis, even), second


def parity(axis):
    return lax.rem(lax.axis_index(axis), 2)


def pick(flag, when_zero, when_one):
    mask = jnp.full(when_zero.shape, flag, jnp.int32) == 0
    return jnp.where(mask, when_zero, when_one)


def dot(left, right, dims=((1,), (0,))):
    return lax.dot_general(left, right, (dims, ((), ())), preferred_element_type=F32)


def cell_onehot(ids):
    cells = lax.broadcasted_iota(jnp.int32, (CELLS, ids.shape[1]), 0)
    return jnp.where(cells == ids, 1.0, 0.0).astype(BF16)


def corner_onehot(row_axis):
    place = lax.broadcasted_iota(jnp.int32, (CELLS, CELLS), row_axis)
    cell = lax.broadcasted_iota(jnp.int32, (CELLS, CELLS), 1 - row_axis)
    corner, row = place >> 6, place & 63
    x = ((row >> 5) << 1) + (corner >> 2)
    y = (((row >> 2) & 7) << 1) + ((corner >> 1) & 1)
    z = ((row & 3) << 1) + (corner & 1)
    return jnp.where(((x * LY + y) * LZ + z) == cell, 1.0, 0.0).astype(BF16)


def shift_z(value, step):
    rows = value.shape[0]
    z = lax.broadcasted_iota(jnp.int32, value.shape, 0) & (LZ - 1)
    if step == 1:
        return jnp.where(z == 0, 0.0, pltpu.roll(value, 1, 0))
    return jnp.where(z == LZ - 1, 0.0, pltpu.roll(value, rows - 1, 0))


def y_sides(dense, hidden_grad):
    def face(near, edge):
        rows = [dense[:, near].reshape(2 * LX * LZ, C), hidden_grad[:, edge].reshape(LX * LZ, C)]
        return jnp.concatenate(rows, 0)

    return face(slice(0, 2), 0), face(slice(LY - 2, LY), LY - 1)


def split_y(rows):
    return rows[: 2 * LX * LZ].reshape(LX, 2 * LZ, C), rows[2 * LX * LZ :].reshape(LX, LZ, C)


def places_kernel(from_ref, to_ref):
    from_ref[...] = corner_onehot(1)
    to_ref[...] = corner_onehot(0)


def build_kernel(place_ref, ids, features, cot, w_down, grid_ref, hidden_ref, even_ref, odd_ref):
    onehot = cell_onehot(ids[...])
    dense = dot(onehot, features[...])
    active = dot(onehot, jnp.ones((onehot.shape[1], C), BF16)) > 0.5
    back_rows = dot(cot[...], w_down[...], ((1,), (1,))).astype(BF16)
    stacked = jnp.concatenate([back_rows[:, k * C : (k + 1) * C] for k in range(8)], 0)
    hidden_grad = jnp.where(active, dot(place_ref[...], stacked), 0.0)
    grid_ref[...] = dense.astype(BF16)
    hidden_ref[...] = hidden_grad.astype(BF16)
    low, high = y_sides(dense.reshape(LX, LY, LZ, C), hidden_grad.reshape(LX, LY, LZ, C))
    side = parity("gy")
    even_ref[...] = pick(side, high, low).astype(BF16)
    odd_ref[...] = pick(side, low, high).astype(BF16)


def y_halos(even_ref, odd_ref):
    even, odd = even_ref[...].astype(F32), odd_ref[...].astype(F32)
    side = parity("gy")
    return split_y(pick(side, odd, even)), split_y(pick(side, even, odd))


def x_sides_kernel(grid_ref, hidden_ref, y_even_ref, y_odd_ref, even_ref, odd_ref):
    plane = LY * LZ
    (low, low_grad), (high, high_grad) = y_halos(y_even_ref, y_odd_ref)

    def face(planes, edge):
        rows = []
        for x in planes:
            rows += [low[x], grid_ref[x * plane : (x + 1) * plane].astype(F32), high[x]]
        rows += [low_grad[edge], hidden_ref[edge * plane : (edge + 1) * plane].astype(F32), high_grad[edge]]
        return jnp.concatenate(rows, 0)

    first, last = face((0, 1), 0), face((LX - 2, LX - 1), LX - 1)
    side = parity("gx")
    even_ref[...] = pick(side, last, first).astype(BF16)
    odd_ref[...] = pick(side, first, last).astype(BF16)


def main_kernel(
    place_ref, ids_ref, grid_ref, hidden_ref, y_even_ref, y_odd_ref, x_even_ref, x_odd_ref, cot_ref, w_down_ref, w_sub,
    coarse_ref, grad_ref, own_ref, send_ref, padded, hidden_pad, sums,
):
    (low, low_grad), (high, high_grad) = y_halos(y_even_ref, y_odd_ref)
    x_even, x_odd = x_even_ref[...].astype(F32), x_odd_ref[...].astype(F32)
    side = parity("gx")
    for rows, at in ((pick(side, x_odd, x_even), 0), (pick(side, x_even, x_odd), LX + 2)):
        split = 2 * (LY + 4) * LZ
        padded[at : at + 2] = rows[:split].reshape(2, LY + 4, LZ, C)
        hidden_pad[0 if at == 0 else LX + 1] = rows[split:].reshape(LY + 2, LZ, C)
    padded[2 : LX + 2, 0:2] = low.reshape(LX, 2, LZ, C)
    padded[2 : LX + 2, LY + 2 :] = high.reshape(LX, 2, LZ, C)
    padded[2 : LX + 2, 2 : LY + 2] = grid_ref[...].astype(F32).reshape(LX, LY, LZ, C)
    hidden_pad[1 : LX + 1, 0] = low_grad
    hidden_pad[1 : LX + 1, LY + 1] = high_grad
    hidden_pad[1 : LX + 1, 1 : LY + 1] = hidden_ref[...].astype(F32).reshape(LX, LY, LZ, C)

    frame = (LX + 2) * (LY + 2) * LZ
    parts = [jnp.zeros((frame, C), F32)] * 3
    for step_x in range(3):
        for step_y in range(3):
            window = padded[step_x : step_x + LX + 2, step_y : step_y + LY + 2].reshape(frame, C).astype(BF16)
            first = step_x * 9 + step_y * 3
            parts = [parts[k] + dot(window, w_sub[first + k]) for k in range(3)]
    pre_act = shift_z(parts[0], 1) + parts[1] + shift_z(parts[2], -1)
    sigmoid = 1.0 / (1.0 + jnp.exp(-pre_act))
    hidden_grad = hidden_pad[...].reshape(frame, C)
    pre_grad = (hidden_grad * sigmoid * (1.0 + pre_act * (1.0 - sigmoid))).astype(BF16)
    grad_ref[...] = pre_grad

    def inner(value):
        return value.reshape(LX + 2, LY + 2, LZ, C)[1 : LX + 1, 1 : LY + 1].reshape(CELLS, C)

    active = dot(cell_onehot(ids_ref[...]), jnp.ones((ids_ref.shape[1], C), BF16)) > 0.5
    hidden = jnp.where(active, inner(pre_act * sigmoid), 0.0).astype(BF16)
    by_corner = dot(place_ref[...], hidden).astype(BF16)
    coarse_input = jnp.concatenate([by_corner[k * U_DEV : (k + 1) * U_DEV] for k in range(8)], 1)
    cot = cot_ref[...]
    coarse_ref[...] = dot(coarse_input, w_down_ref[...]).astype(BF16)
    grad = inner(pre_grad.astype(F32))
    spread = jnp.concatenate([shift_z(grad, -1), grad, shift_z(grad, 1)], 1).astype(BF16)
    for step_x in range(3):
        for step_y in range(3):
            first = (step_x * 9 + step_y * 3) * C
            window = padded[step_x + 1 : step_x + 1 + LX, step_y + 1 : step_y + 1 + LY]
            taps = dot(window.reshape(CELLS, C).astype(BF16), spread, ((0,), (0,)))
            for k in range(3):
                sums[first + k * C : first + (k + 1) * C] = taps[:, k * C : (k + 1) * C]
    down = dot(coarse_input, cot, ((0,), (0,)))
    base = OFFSETS * C
    sums[base : base + 8 * C] = down[:, :C]
    sums[base + 8 * C : base + 16 * C] = down[:, C:]
    sums[base + 16 * C :] = jnp.zeros((2 * HALF - base - 16 * C, C), F32)
    mine, other = halves()
    own_ref[...] = sums[mine].astype(BF16)
    send_ref[...] = sums[other].astype(BF16)


def halves():
    core = parity("gx")
    return pl.ds(pl.multiple_of(core * HALF, HALF), HALF), pl.ds(pl.multiple_of((1 - core) * HALF, HALF), HALF)


def feature_kernel(ids_ref, grad_ref, w_sub_ref, out_ref, padded):
    padded[...] = grad_ref[...].astype(F32).reshape(LX + 2, LY + 2, LZ, C)
    parts = [jnp.zeros((CELLS, C), F32)] * 3
    for step_x in range(3):
        for step_y in range(3):
            window = padded[2 - step_x : 2 - step_x + LX, 2 - step_y : 2 - step_y + LY]
            window = window.reshape(CELLS, C).astype(BF16)
            first = step_x * 9 + step_y * 3
            parts = [parts[k] + dot(window, w_sub_ref[first + k], ((1,), (1,))) for k in range(3)]
    total = shift_z(parts[0], -1) + parts[1] + shift_z(parts[2], 1)
    out_ref[...] = dot(cell_onehot(ids_ref[...]), total.astype(BF16), ((0,), (0,))).astype(BF16)


def add_kernel(own_ref, other_ref, out_ref):
    out_ref[...] = (own_ref[...].astype(F32) + other_ref[...].astype(F32)).astype(BF16)


def sum_kernel(parts_ref, out_ref):
    total = parts_ref[:CHUNK].astype(F32)
    for start in range(CHUNK, parts_ref.shape[0], CHUNK):
        total = total + parts_ref[start : start + CHUNK].astype(F32)
    total = total.astype(BF16)
    for start in range(0, out_ref.shape[0], CHUNK):
        out_ref[start : start + CHUNK] = total


def unpack_kernel(own_ref, other_ref, sub_ref, down_ref, sums):
    mine, other = halves()
    sums[mine] = own_ref[...].astype(F32)
    sums[other] = other_ref[...].astype(F32)
    base = OFFSETS * C
    sub_ref[...] = sums[:base].reshape(OFFSETS, C, C)
    down_ref[:, :C] = sums[base : base + 8 * C]
    down_ref[:, C:] = sums[base + 8 * C : base + 16 * C]


def call(kernel, outs, scratch=(), flops=0):
    return pl.pallas_call(
        kernel,
        out_shape=[jax.ShapeDtypeStruct(*out) for out in outs],
        scratch_shapes=list(scratch),
        cost_estimate=pl.CostEstimate(flops=flops, bytes_accessed=1 << 20, transcendentals=0),
        compiler_params=pltpu.CompilerParams(vmem_limit_bytes=40 * 1024 * 1024),
    )


def core_swap(value):
    return lax.ppermute(value, "gx", swap_pairs(lax.axis_size("gx"))[0])


def reduce_all(own, send):
    rows, cols = lax.axis_size("gx"), lax.axis_size("gy")
    plane = [
        [i * cols + j for i in range(core, rows, 2) for j in (first, first + 1)]
        for core in range(2)
        for first in range(0, cols, 2)
    ]
    depth = [[i * cols + j for j in range(side, cols, 2)] for i in range(rows) for side in range(2)]

    def trade(value, groups):
        return lax.all_to_all(value, AXES, 0, 0, axis_index_groups=groups, tiled=True)

    packed = ((HALF, C), BF16)
    (part,) = call(add_kernel, [packed])(own, core_swap(send))
    (mine,) = call(sum_kernel, [((len(depth[0]) * CHUNK, C), BF16)])(trade(part, plane))
    (total,) = call(sum_kernel, [packed])(trade(mine, depth))
    whole = trade(total, plane)
    return whole, core_swap(whole)


def local(features, w_sub, w_down, cell_ids, send_rows, map_in, map_out, cotangent):
    ids = cell_ids[None]
    rows = features.shape[0]
    dense = ((CELLS, C), BF16)
    y_side = ((3 * LX * LZ, C), BF16)
    x_side = (((2 * (LY + 4) + LY + 2) * LZ, C), BF16)
    frame = (((LX + 2) * (LY + 2) * LZ, C), BF16)
    packed = ((HALF, C), BF16)
    framed = pltpu.VMEM((LX + 2, LY + 2, LZ, C), F32)
    padded = pltpu.VMEM((LX + 4, LY + 4, LZ, C), F32)
    sums = pltpu.VMEM((2 * HALF, C), F32)

    place = ((CELLS, CELLS), BF16)
    from_corner, to_corner = call(places_kernel, [place, place], flops=LONG)()
    grid, hidden_grad, y_even, y_odd = call(build_kernel, [dense, dense, y_side, y_side], flops=LONG)(
        from_corner, ids, features, cotangent, w_down
    )
    y_even, y_odd = swap_both(y_even, y_odd, "gy")
    sides = call(x_sides_kernel, [x_side, x_side], flops=LONG)(grid, hidden_grad, y_even, y_odd)
    x_even, x_odd = swap_both(*sides, "gx")
    coarse, grad, own, send = call(
        main_kernel,
        [((U_DEV, C2), BF16), frame, packed, packed],
        [padded, framed, sums],
        1 << 31,
    )(to_corner, ids, grid, hidden_grad, y_even, y_odd, x_even, x_odd, cotangent, w_down, w_sub)
    (feature_grad,) = call(feature_kernel, [((rows, C), BF16)], [framed], flops=1 << 30)(ids, grad, w_sub)
    sub_grad, down_grad = call(
        unpack_kernel, [((OFFSETS, C, C), F32), ((8 * C, C2), F32)], [sums]
    )(*reduce_all(own, send))
    return coarse, feature_grad, sub_grad, down_grad


def solution(mesh):
    rows = P(AXES, None)
    flat = P(AXES)
    maps = P(None, AXES)
    return jax.shard_map(
        local,
        mesh=mesh,
        in_specs=(rows, P(), P(), flat, flat, maps, maps, rows),
        out_specs=(rows, rows, P(), P()),
        check_vma=False,
    )
```

```python
import functools

import jax
import jax.numpy as jnp
from jax import lax
from jax.experimental import pallas as pl
from jax.experimental.pallas import tpu as pltpu
from jax.sharding import PartitionSpec as P

LX = 4
LY = 16
LZ = 8
CELLS = LX * LY * LZ
U_DEV = 64
C = 128
C2 = 256
OFFSETS = 27
AXES = ("gx", "gy")
CHUNK = 176
HALF = 16 * CHUNK
LONG = 1 << 33

F32 = jnp.float32
BF16 = jnp.bfloat16


def swap_pairs(count):
    even = [(k, k ^ 1) for k in range(count)]
    odd = [(k, k + 1 if k % 2 else k - 1) for k in range(count)]
    return even, [(k, m) for k, m in odd if 0 <= m < count]


def swap_both(first, second, axis):
    even, odd = swap_pairs(lax.axis_size(axis))
    second = lax.ppermute(second, axis, odd)
    return lax.ppermute(first, axis, even), second


def parity(axis):
    return lax.rem(lax.axis_index(axis), 2)


def pick(flag, when_zero, when_one):
    mask = jnp.full(when_zero.shape, flag, jnp.int32) == 0
    return jnp.where(mask, when_zero, when_one)


def dot(left, right, dims=((1,), (0,))):
    return lax.dot_general(left, right, (dims, ((), ())), preferred_element_type=F32)


def cell_onehot(ids):
    cells = lax.broadcasted_iota(jnp.int32, (CELLS, ids.shape[1]), 0)
    return jnp.where(cells == ids, 1.0, 0.0).astype(BF16)


def corner_onehot(row_axis):
    place = lax.broadcasted_iota(jnp.int32, (CELLS, CELLS), row_axis)
    cell = lax.broadcasted_iota(jnp.int32, (CELLS, CELLS), 1 - row_axis)
    corner, row = place >> 6, place & 63
    x = ((row >> 5) << 1) + (corner >> 2)
    y = (((row >> 2) & 7) << 1) + ((corner >> 1) & 1)
    z = ((row & 3) << 1) + (corner & 1)
    return jnp.where(((x * LY + y) * LZ + z) == cell, 1.0, 0.0).astype(BF16)


def shift_z(value, step):
    rows = value.shape[0]
    z = lax.broadcasted_iota(jnp.int32, value.shape, 0) & (LZ - 1)
    if step == 1:
        return jnp.where(z == 0, 0.0, pltpu.roll(value, 1, 0))
    return jnp.where(z == LZ - 1, 0.0, pltpu.roll(value, rows - 1, 0))


def y_sides(dense, hidden_grad):
    def face(near, edge):
        rows = [dense[:, near].reshape(2 * LX * LZ, C), hidden_grad[:, edge].reshape(LX * LZ, C)]
        return jnp.concatenate(rows, 0)

    return face(slice(0, 2), 0), face(slice(LY - 2, LY), LY - 1)


def split_y(rows):
    return rows[: 2 * LX * LZ].reshape(LX, 2 * LZ, C), rows[2 * LX * LZ :].reshape(LX, LZ, C)


def places_kernel(from_ref, to_ref):
    from_ref[...] = corner_onehot(1)
    to_ref[...] = corner_onehot(0)


def build_kernel(place_ref, ids, features, cot, w_down, grid_ref, hidden_ref, even_ref, odd_ref):
    onehot = cell_onehot(ids[...])
    dense = dot(onehot, features[...])
    active = dot(onehot, jnp.ones((onehot.shape[1], C), BF16)) > 0.5
    back_rows = dot(cot[...], w_down[...], ((1,), (1,))).astype(BF16)
    stacked = jnp.concatenate([back_rows[:, k * C : (k + 1) * C] for k in range(8)], 0)
    hidden_grad = jnp.where(active, dot(place_ref[...], stacked), 0.0)
    grid_ref[...] = dense.astype(BF16)
    hidden_ref[...] = hidden_grad.astype(BF16)
    low, high = y_sides(dense.reshape(LX, LY, LZ, C), hidden_grad.reshape(LX, LY, LZ, C))
    side = parity("gy")
    even_ref[...] = pick(side, high, low).astype(BF16)
    odd_ref[...] = pick(side, low, high).astype(BF16)


def y_halos(odd_ref, even_ref):
    even, odd = even_ref[...].astype(F32), odd_ref[...].astype(F32)
    side = parity("gy")
    return split_y(pick(side, odd, even)), split_y(pick(side, even, odd))


def x_sides_kernel(grid_ref, hidden_ref, y_odd_ref, y_even_ref, even_ref, odd_ref):
    plane = LY * LZ
    (low, low_grad), (high, high_grad) = y_halos(y_odd_ref, y_even_ref)

    def face(planes, edge):
        rows = []
        for x in planes:
            rows += [low[x], grid_ref[x * plane : (x + 1) * plane].astype(F32), high[x]]
        rows += [low_grad[edge], hidden_ref[edge * plane : (edge + 1) * plane].astype(F32), high_grad[edge]]
        return jnp.concatenate(rows, 0)

    first, last = face((0, 1), 0), face((LX - 2, LX - 1), LX - 1)
    side = parity("gx")
    even_ref[...] = pick(side, last, first).astype(BF16)
    odd_ref[...] = pick(side, first, last).astype(BF16)


def main_kernel(
    place_ref, ids_ref, grid_ref, hidden_ref, y_odd_ref, y_even_ref, x_odd_ref, x_even_ref, cot_ref, w_down_ref, w_sub,
    coarse_ref, grad_ref, own_ref, send_ref, padded, hidden_pad, sums,
):
    (low, low_grad), (high, high_grad) = y_halos(y_odd_ref, y_even_ref)
    x_even, x_odd = x_even_ref[...].astype(F32), x_odd_ref[...].astype(F32)
    side = parity("gx")
    for rows, at in ((pick(side, x_odd, x_even), 0), (pick(side, x_even, x_odd), LX + 2)):
        split = 2 * (LY + 4) * LZ
        padded[at : at + 2] = rows[:split].reshape(2, LY + 4, LZ, C)
        hidden_pad[0 if at == 0 else LX + 1] = rows[split:].reshape(LY + 2, LZ, C)
    padded[2 : LX + 2, 0:2] = low.reshape(LX, 2, LZ, C)
    padded[2 : LX + 2, LY + 2 :] = high.reshape(LX, 2, LZ, C)
    padded[2 : LX + 2, 2 : LY + 2] = grid_ref[...].astype(F32).reshape(LX, LY, LZ, C)
    hidden_pad[1 : LX + 1, 0] = low_grad
    hidden_pad[1 : LX + 1, LY + 1] = high_grad
    hidden_pad[1 : LX + 1, 1 : LY + 1] = hidden_ref[...].astype(F32).reshape(LX, LY, LZ, C)

    frame = (LX + 2) * (LY + 2) * LZ
    parts = [jnp.zeros((frame, C), F32)] * 3
    for step_x in range(3):
        for step_y in range(3):
            window = padded[step_x : step_x + LX + 2, step_y : step_y + LY + 2].reshape(frame, C).astype(BF16)
            first = step_x * 9 + step_y * 3
            parts = [parts[k] + dot(window, w_sub[first + k]) for k in range(3)]
    pre_act = shift_z(parts[0], 1) + parts[1] + shift_z(parts[2], -1)
    sigmoid = 1.0 / (1.0 + jnp.exp(-pre_act))
    hidden_grad = hidden_pad[...].reshape(frame, C)
    pre_grad = (hidden_grad * sigmoid * (1.0 + pre_act * (1.0 - sigmoid))).astype(BF16)
    grad_ref[...] = pre_grad

    def inner(value):
        return value.reshape(LX + 2, LY + 2, LZ, C)[1 : LX + 1, 1 : LY + 1].reshape(CELLS, C)

    active = dot(cell_onehot(ids_ref[...]), jnp.ones((ids_ref.shape[1], C), BF16)) > 0.5
    hidden = jnp.where(active, inner(pre_act * sigmoid), 0.0).astype(BF16)
    by_corner = dot(place_ref[...], hidden).astype(BF16)
    coarse_input = jnp.concatenate([by_corner[k * U_DEV : (k + 1) * U_DEV] for k in range(8)], 1)
    cot = cot_ref[...]
    coarse_ref[...] = dot(coarse_input, w_down_ref[...]).astype(BF16)
    grad = inner(pre_grad.astype(F32))
    spread = jnp.concatenate([shift_z(grad, -1), grad, shift_z(grad, 1)], 1).astype(BF16)
    for step_x in range(3):
        for step_y in range(3):
            first = (step_x * 9 + step_y * 3) * C
            window = padded[step_x + 1 : step_x + 1 + LX, step_y + 1 : step_y + 1 + LY]
            taps = dot(window.reshape(CELLS, C).astype(BF16), spread, ((0,), (0,)))
            for k in range(3):
                sums[first + k * C : first + (k + 1) * C] = taps[:, k * C : (k + 1) * C]
    down = dot(coarse_input, cot, ((0,), (0,)))
    base = OFFSETS * C
    sums[base : base + 8 * C] = down[:, :C]
    sums[base + 8 * C : base + 16 * C] = down[:, C:]
    sums[base + 16 * C :] = jnp.zeros((2 * HALF - base - 16 * C, C), F32)
    mine, other = halves()
    own_ref[...] = sums[mine].astype(BF16)
    send_ref[...] = sums[other].astype(BF16)


def halves():
    core = parity("gx")
    return pl.ds(pl.multiple_of(core * HALF, HALF), HALF), pl.ds(pl.multiple_of((1 - core) * HALF, HALF), HALF)


def feature_kernel(ids_ref, grad_ref, w_sub_ref, out_ref, done_ref, padded):
    done_ref[...] = jnp.zeros_like(done_ref)
    padded[...] = grad_ref[...].astype(F32).reshape(LX + 2, LY + 2, LZ, C)
    parts = [jnp.zeros((CELLS, C), F32)] * 3
    for step_x in range(3):
        for step_y in range(3):
            window = padded[2 - step_x : 2 - step_x + LX, 2 - step_y : 2 - step_y + LY]
            window = window.reshape(CELLS, C).astype(BF16)
            first = step_x * 9 + step_y * 3
            parts = [parts[k] + dot(window, w_sub_ref[first + k], ((1,), (1,))) for k in range(3)]
    total = shift_z(parts[0], -1) + parts[1] + shift_z(parts[2], 1)
    out_ref[...] = dot(cell_onehot(ids_ref[...]), total.astype(BF16), ((0,), (0,))).astype(BF16)


def add_kernel(own_ref, other_ref, out_ref):
    out_ref[...] = (own_ref[...].astype(F32) + other_ref[...].astype(F32)).astype(BF16)


def sum_kernel(parts_ref, out_ref):
    total = parts_ref[:CHUNK].astype(F32)
    for start in range(CHUNK, parts_ref.shape[0], CHUNK):
        total = total + parts_ref[start : start + CHUNK].astype(F32)
    total = total.astype(BF16)
    for start in range(0, out_ref.shape[0], CHUNK):
        out_ref[start : start + CHUNK] = total


def pair_kernel(own_ref, other_ref, *refs):
    out_ref = refs[-1]
    total = (own_ref[...].astype(F32) + other_ref[...].astype(F32)).astype(BF16)
    for start in range(0, out_ref.shape[0], CHUNK):
        out_ref[start : start + CHUNK] = total


def unpack_kernel(other, data_ref, *refs):
    sub_hbm, down_hbm, blocks, down, sems = refs[-5:]
    held = parity("gx") ^ other
    blocks[...] = data_ref[...].astype(F32).reshape(HALF // C, C, C)
    first = HALF // C

    @pl.when(held == 0)
    def _():
        copy = pltpu.make_async_copy(blocks, sub_hbm.at[:first], sems.at[0])
        copy.start()
        copy.wait()

    @pl.when(held == 1)
    def _():
        rest = OFFSETS - first
        copy = pltpu.make_async_copy(blocks.at[:rest], sub_hbm.at[first:], sems.at[0])
        copy.start()
        for k in range(2):
            down[:, k * C : (k + 1) * C] = blocks[rest + 8 * k : rest + 8 * (k + 1)].reshape(8 * C, C)
        second = pltpu.make_async_copy(down, down_hbm, sems.at[1])
        second.start()
        copy.wait()
        second.wait()


def call(kernel, outs, scratch=(), flops=0, **options):
    return pl.pallas_call(
        kernel,
        out_shape=[jax.ShapeDtypeStruct(*out) for out in outs],
        scratch_shapes=list(scratch),
        cost_estimate=pl.CostEstimate(flops=flops, bytes_accessed=1 << 20, transcendentals=0),
        compiler_params=pltpu.CompilerParams(vmem_limit_bytes=40 * 1024 * 1024),
        **options,
    )


def core_swap(value):
    return lax.ppermute(value, "gx", swap_pairs(lax.axis_size("gx"))[0])


def reduce_all(own, send, after):
    rows, cols = lax.axis_size("gx"), lax.axis_size("gy")
    plane = [
        [i * cols + j for i in range(core, rows, 2) for j in (first, first + 1)]
        for core in range(2)
        for first in range(0, cols, 2)
    ]

    def trade(value, groups):
        return lax.all_to_all(value, AXES, 0, 0, axis_index_groups=groups, tiled=True)

    packed = ((HALF, C), BF16)
    (part,) = call(add_kernel, [packed])(own, core_swap(send))
    (total,) = call(sum_kernel, [((CHUNK, C), BF16)])(trade(part, plane))
    for flip in (1, 2, 7):
        pairs = [(j, ((j >> 1) ^ flip) * 2 + (j & 1)) for j in range(cols)]
        copies = HALF if flip == 7 else CHUNK
        extra = (after,) if flip == 2 else ()
        (total,) = call(pair_kernel, [((copies, C), BF16)])(total, lax.ppermute(total, "gy", pairs), *extra)
    whole = trade(total, plane)
    return whole, core_swap(whole)


def local(features, w_sub, w_down, cell_ids, send_rows, map_in, map_out, cotangent):
    ids = cell_ids[None]
    rows = features.shape[0]
    dense = ((CELLS, C), BF16)
    y_side = ((3 * LX * LZ, C), BF16)
    x_side = (((2 * (LY + 4) + LY + 2) * LZ, C), BF16)
    frame = (((LX + 2) * (LY + 2) * LZ, C), BF16)
    packed = ((HALF, C), BF16)
    framed = pltpu.VMEM((LX + 2, LY + 2, LZ, C), F32)
    padded = pltpu.VMEM((LX + 4, LY + 4, LZ, C), F32)
    sums = pltpu.VMEM((2 * HALF, C), F32)

    place = ((CELLS, CELLS), BF16)
    from_corner, to_corner = call(places_kernel, [place, place], flops=LONG)()
    grid, hidden_grad, y_even, y_odd = call(build_kernel, [dense, dense, y_side, y_side], flops=LONG)(
        from_corner, ids, features, cotangent, w_down
    )
    y_even, y_odd = swap_both(y_even, y_odd, "gy")
    sides = call(x_sides_kernel, [x_side, x_side], flops=LONG)(grid, hidden_grad, y_odd, y_even)
    x_even, x_odd = swap_both(*sides, "gx")
    coarse, grad, own, send = call(
        main_kernel,
        [((U_DEV, C2), BF16), frame, packed, packed],
        [padded, framed, sums],
        1 << 31,
    )(to_corner, ids, grid, hidden_grad, y_odd, y_even, x_odd, x_even, cotangent, w_down, w_sub)
    feature_grad, done = call(feature_kernel, [((rows, C), BF16), ((16, C), BF16)], [framed], flops=LONG)(ids, grad, w_sub)
    whole, other = reduce_all(own, send, done)
    grads = [((OFFSETS, C, C), F32), ((8 * C, C2), F32)]
    scratch = [pltpu.VMEM((HALF // C, C, C), F32), pltpu.VMEM((8 * C, C2), F32), pltpu.SemaphoreType.DMA((2,))]
    in_hbm = [pl.BlockSpec(memory_space=pltpu.HBM)] * 2
    grads_own = call(functools.partial(unpack_kernel, 0), grads, scratch, LONG, out_specs=in_hbm)(whole)
    sub_grad, down_grad = call(
        functools.partial(unpack_kernel, 1),
        grads,
        scratch,
        in_specs=[pl.BlockSpec(memory_space=pltpu.VMEM), *in_hbm],
        out_specs=in_hbm,
        input_output_aliases={1: 0, 2: 1},
    )(other, *grads_own)
    return coarse, feature_grad, sub_grad, down_grad


def solution(mesh):
    rows = P(AXES, None)
    flat = P(AXES)
    maps = P(None, AXES)
    return jax.shard_map(
        local,
        mesh=mesh,
        in_specs=(rows, P(), P(), flat, flat, maps, maps, rows),
        out_specs=(rows, rows, P(), P()),
        check_vma=False,
    )
```

```python
import functools

import jax
import jax.numpy as jnp
from jax import lax
from jax.experimental import pallas as pl
from jax.experimental.pallas import tpu as pltpu
from jax.sharding import PartitionSpec as P

LX = 4
LY = 16
LZ = 8
CELLS = LX * LY * LZ
U_DEV = 64
C = 128
C2 = 256
OFFSETS = 27
AXES = ("gx", "gy")
CHUNK = 176
HALF = 16 * CHUNK
LONG = 1 << 33

F32 = jnp.float32
BF16 = jnp.bfloat16


def swap_pairs(count):
    even = [(k, k ^ 1) for k in range(count)]
    odd = [(k, k + 1 if k % 2 else k - 1) for k in range(count)]
    return even, [(k, m) for k, m in odd if 0 <= m < count]


def swap(value, axis, kind):
    return lax.ppermute(value, axis, swap_pairs(lax.axis_size(axis))[kind])


def swap_both(first, second, axis):
    second = swap(second, axis, 1)
    return swap(first, axis, 0), second


def parity(axis):
    return lax.rem(lax.axis_index(axis), 2)


def pick(flag, when_zero, when_one):
    mask = jnp.full(when_zero.shape, flag, jnp.int32) == 0
    return jnp.where(mask, when_zero, when_one)


def dot(left, right, dims=((1,), (0,))):
    return lax.dot_general(left, right, (dims, ((), ())), preferred_element_type=F32)


def cell_onehot(ids):
    cells = lax.broadcasted_iota(jnp.int32, (CELLS, ids.shape[1]), 0)
    return jnp.where(cells == ids, 1.0, 0.0).astype(BF16)


def corner_onehot(row_axis):
    place = lax.broadcasted_iota(jnp.int32, (CELLS, CELLS), row_axis)
    cell = lax.broadcasted_iota(jnp.int32, (CELLS, CELLS), 1 - row_axis)
    corner, row = place >> 6, place & 63
    x = ((row >> 5) << 1) + (corner >> 2)
    y = (((row >> 2) & 7) << 1) + ((corner >> 1) & 1)
    z = ((row & 3) << 1) + (corner & 1)
    return jnp.where(((x * LY + y) * LZ + z) == cell, 1.0, 0.0).astype(BF16)


def shift_z(value, step):
    rows = value.shape[0]
    z = lax.broadcasted_iota(jnp.int32, value.shape, 0) & (LZ - 1)
    if step == 1:
        return jnp.where(z == 0, 0.0, pltpu.roll(value, 1, 0))
    return jnp.where(z == LZ - 1, 0.0, pltpu.roll(value, rows - 1, 0))


def y_sides(dense, hidden_grad):
    def face(near, edge):
        rows = [dense[:, near].reshape(2 * LX * LZ, C), hidden_grad[:, edge].reshape(LX * LZ, C)]
        return jnp.concatenate(rows, 0)

    return face(slice(0, 2), 0), face(slice(LY - 2, LY), LY - 1)


def split_y(rows):
    return rows[: 2 * LX * LZ].reshape(LX, 2 * LZ, C), rows[2 * LX * LZ :].reshape(LX, LZ, C)


def places_kernel(from_ref, to_ref):
    from_ref[...] = corner_onehot(1)
    to_ref[...] = corner_onehot(0)


def build_kernel(place_ref, ids, features, cot, w_down, grid_ref, hidden_ref, even_ref, odd_ref, x_odd_ref):
    onehot = cell_onehot(ids[...])
    dense = dot(onehot, features[...])
    active = dot(onehot, jnp.ones((onehot.shape[1], C), BF16)) > 0.5
    back_rows = dot(cot[...], w_down[...], ((1,), (1,))).astype(BF16)
    stacked = jnp.concatenate([back_rows[:, k * C : (k + 1) * C] for k in range(8)], 0)
    hidden_grad = jnp.where(active, dot(place_ref[...], stacked), 0.0)
    grid_ref[...] = dense.astype(BF16)
    hidden_ref[...] = hidden_grad.astype(BF16)
    low, high = y_sides(dense.reshape(LX, LY, LZ, C), hidden_grad.reshape(LX, LY, LZ, C))
    side = parity("gy")
    even_ref[...] = pick(side, high, low).astype(BF16)
    odd_ref[...] = pick(side, low, high).astype(BF16)
    first = x_face(dense, hidden_grad, 0)
    last = x_face(dense, hidden_grad, LX - 1)
    x_odd_ref[...] = pick(parity("gx"), first, last).astype(BF16)


def x_face(dense, hidden_grad, edge):
    plane = LY * LZ
    near = dense[: 2 * plane] if edge == 0 else dense[CELLS - 2 * plane :]
    return jnp.concatenate([near, hidden_grad[edge * plane : (edge + 1) * plane]], 0)


def y_halos(odd_ref, even_ref):
    even, odd = even_ref[...].astype(F32), odd_ref[...].astype(F32)
    side = parity("gy")
    return split_y(pick(side, odd, even)), split_y(pick(side, even, odd))


def x_sides_kernel(grid_ref, hidden_ref, y_odd_ref, y_even_ref, even_ref, odd_ref):
    (low, low_grad), (high, high_grad) = y_halos(y_odd_ref, y_even_ref)

    def corners(near, edge):
        rows = []
        for x in near:
            rows += [low[x], high[x]]
        return jnp.concatenate([*rows, low_grad[edge], high_grad[edge]], 0)

    first, last = corners((0, 1), 0), corners((LX - 2, LX - 1), LX - 1)
    dense, hidden_grad = grid_ref[...].astype(F32), hidden_ref[...].astype(F32)
    side = parity("gx")
    face = pick(side, x_face(dense, hidden_grad, LX - 1), x_face(dense, hidden_grad, 0))
    even_ref[...] = jnp.concatenate([face, pick(side, last, first)], 0).astype(BF16)
    odd_ref[...] = pick(side, first, last).astype(BF16)


def store_side(planes, rows):
    face, corner = 2 * LY * LZ, 3 * LY * LZ
    planes[:, 2 : LY + 2] = rows[:face].reshape(2, LY, LZ, C)
    ends = rows[corner : corner + 8 * LZ].reshape(2, 4, LZ, C)
    planes[:, 0:2] = ends[:, 0:2]
    planes[:, LY + 2 :] = ends[:, 2:4]
    grads = corner + 8 * LZ
    return jnp.concatenate([rows[grads : grads + LZ], rows[face:corner], rows[grads + LZ :]], 0)


def kernel_rows(w_sub, step_x):
    rows = []
    for step_y in range(3):
        first = step_x * 9 + step_y * 3
        rows.append(jnp.concatenate([w_sub[first + k] for k in range(3)], 1))
    return jnp.concatenate(rows, 0)


def frame_rows(planes):
    rows = planes.shape[0] * (LY + 2) * LZ
    return jnp.concatenate([planes[:, k : k + LY + 2].reshape(rows, C).astype(BF16) for k in range(3)], 1)


def fold(taps):
    return shift_z(taps[:, :C], 1) + taps[:, C : 2 * C] + shift_z(taps[:, 2 * C :], -1)


def unfold(grad):
    return jnp.concatenate([shift_z(grad, -1), grad, shift_z(grad, 1)], 1).astype(BF16)


def activate(pre_act, hidden_grad):
    sigmoid = 1.0 / (1.0 + jnp.exp(-pre_act))
    pre_grad = hidden_grad * sigmoid * (1.0 + pre_act * (1.0 - sigmoid))
    return pre_act * sigmoid, pre_grad.astype(BF16)


def inner_rows(value):
    return value[:, 1 : LY + 1].reshape(value.shape[0] * LY * LZ, C)


def early_kernel(grid_ref, hidden_ref, y_odd_ref, y_even_ref, w_sub, mid, hidden_mid, pre_ref, taps_ref):
    (low, low_grad), (high, high_grad) = y_halos(y_odd_ref, y_even_ref)
    mid[:, 0:2] = low.reshape(LX, 2, LZ, C)
    mid[:, LY + 2 :] = high.reshape(LX, 2, LZ, C)
    mid[:, 2 : LY + 2] = grid_ref[...].astype(F32).reshape(LX, LY, LZ, C)
    hidden_mid[:, 0] = low_grad
    hidden_mid[:, LY + 1] = high_grad
    hidden_mid[:, 1 : LY + 1] = hidden_ref[...].astype(F32).reshape(LX, LY, LZ, C)
    rows = frame_rows(mid[...])
    pre_ref[...] = jnp.zeros_like(pre_ref)
    for step_x in range(3):
        part = fold(dot(rows, kernel_rows(w_sub, step_x)))
        pre_ref[2 - step_x : 2 - step_x + LX] += part.reshape(LX, LY + 2, LZ, C)
    _, grad = activate(inner_rows(pre_ref[2:4]), inner_rows(hidden_mid[1:3]))
    spread = unfold(grad.astype(F32))
    for group in range(9):
        step_x, step_y = group // 3, group % 3
        window = mid[step_x : step_x + 2, step_y + 1 : step_y + 1 + LY].reshape(2 * LY * LZ, C)
        taps = dot(window.astype(BF16), spread, ((0,), (0,)))
        for k in range(3):
            taps_ref[(3 * group + k) * C : (3 * group + k + 1) * C] = taps[:, k * C : (k + 1) * C]


def store_half(half, out_ref, mid, side, spread_ref, hidden_ref, place_ref, cot, taps_ref):
    blocks = HALF // C

    def plane(x, step_y):
        source = side[x + 2 if x < 0 else x - 2] if x < 0 or x >= LX else mid[x]
        return source[step_y + 1 : step_y + 1 + LY].reshape(LY * LZ, C)

    for group in range(8) if half == 0 else (7, 8):
        step_x, step_y = group // 3, group % 3
        held = [k for k in range(3) if (3 * group + k) // blocks == half]
        window = jnp.concatenate([plane(step_x - 1, step_y), plane(LX + step_x - 2, step_y)], 0)
        spread = spread_ref[:, held[0] * C : (held[-1] + 1) * C]
        taps = dot(window.astype(BF16), spread, ((0,), (0,)))
        for k in held:
            block = 3 * group + k
            total = taps[:, (k - held[0]) * C : (k - held[0] + 1) * C] + taps_ref[block * C : (block + 1) * C]
            at = (block - half * blocks) * C
            out_ref[at : at + C] = total.astype(BF16)
    if half == 1:
        down = dot(coarse_rows(place_ref, hidden_ref), cot[...], ((0,), (0,))).astype(BF16)
        at = (OFFSETS - blocks) * C
        out_ref[at : at + 8 * C] = down[:, :C]
        out_ref[at + 8 * C : at + 16 * C] = down[:, C:]
        out_ref[at + 16 * C :] = jnp.zeros((HALF - at - 16 * C, C), BF16)


def coarse_rows(place_ref, hidden_ref):
    by_corner = dot(place_ref[...], hidden_ref[...]).astype(BF16)
    return jnp.concatenate([by_corner[k * U_DEV : (k + 1) * U_DEV] for k in range(8)], 1)


def store_of(other, out_ref, *refs):
    held = parity("gx") ^ other
    for half in range(2):
        pl.when(held == half)(functools.partial(store_half, half, out_ref, *refs))


def main_kernel(
    place_ref, ids_ref, mid, hidden_mid, pre_ref, taps_ref, x_odd_ref, x_ends_ref, x_even_ref, cot_ref, w_sub,
    send_ref, grad_ref, spread_ref, hidden_ref, side,
):
    x_odd = jnp.concatenate([x_odd_ref[...].astype(F32), x_ends_ref[...].astype(F32)], 0)
    x_even = x_even_ref[...].astype(F32)
    flag = parity("gx")
    low_grad = store_side(side.at[0:2], pick(flag, x_odd, x_even))
    high_grad = store_side(side.at[2:4], pick(flag, x_even, x_odd))
    column = (LY + 2) * LZ
    centre = kernel_rows(w_sub, 1)
    rows = frame_rows(side[0:2])
    outer = fold(dot(rows, kernel_rows(w_sub, 0)))
    first = pre_ref[0].reshape(column, C) + outer[:column] + fold(dot(rows[column:], centre))
    second = pre_ref[1].reshape(column, C) + outer[column:]
    rows = frame_rows(side[2:4])
    outer = fold(dot(rows, kernel_rows(w_sub, 2)))
    last = pre_ref[LX + 1].reshape(column, C) + outer[column:] + fold(dot(rows[:column], centre))
    before = pre_ref[LX].reshape(column, C) + outer[:column]
    pre_act = jnp.concatenate([first, second, pre_ref[2:LX].reshape(2 * column, C), before, last], 0)
    hidden_grad = jnp.concatenate([low_grad, hidden_mid[...].reshape(LX * column, C), high_grad], 0)
    hidden, pre_grad = activate(pre_act, hidden_grad)
    grad_ref[...] = pre_grad

    def framed(value):
        return value.reshape(LX + 2, LY + 2, LZ, C)

    grad = framed(pre_grad.astype(F32))
    spread_ref[...] = unfold(inner_rows(jnp.concatenate([grad[1:2], grad[LX : LX + 1]], 0)))
    active = dot(cell_onehot(ids_ref[...]), jnp.ones((ids_ref.shape[1], C), BF16)) > 0.5
    hidden_ref[...] = jnp.where(active, inner_rows(framed(hidden)[1 : LX + 1]), 0.0).astype(BF16)
    store_of(1, send_ref, mid, side, spread_ref, hidden_ref, place_ref, cot_ref, taps_ref)


def late_kernel(place_ref, mid, side, spread_ref, hidden_ref, cot_ref, taps_ref, w_down_ref, own_ref, coarse_ref):
    coarse_ref[...] = dot(coarse_rows(place_ref, hidden_ref), w_down_ref[...]).astype(BF16)
    store_of(0, own_ref, mid, side, spread_ref, hidden_ref, place_ref, cot_ref, taps_ref)


def feature_kernel(ids_ref, grad_ref, w_sub_ref, out_ref, done_ref, padded):
    done_ref[...] = jnp.zeros_like(done_ref)
    padded[...] = grad_ref[...].astype(F32).reshape(LX + 2, LY + 2, LZ, C)
    parts = [jnp.zeros((CELLS, C), F32)] * 3
    for step_x in range(3):
        for step_y in range(3):
            window = padded[2 - step_x : 2 - step_x + LX, 2 - step_y : 2 - step_y + LY]
            window = window.reshape(CELLS, C).astype(BF16)
            first = step_x * 9 + step_y * 3
            parts = [parts[k] + dot(window, w_sub_ref[first + k], ((1,), (1,))) for k in range(3)]
    total = shift_z(parts[0], -1) + parts[1] + shift_z(parts[2], 1)
    out_ref[...] = dot(cell_onehot(ids_ref[...]), total.astype(BF16), ((0,), (0,))).astype(BF16)


def add_kernel(own_ref, other_ref, out_ref):
    out_ref[...] = (own_ref[...].astype(F32) + other_ref[...].astype(F32)).astype(BF16)


def sum_kernel(parts_ref, out_ref):
    total = parts_ref[:CHUNK].astype(F32)
    for start in range(CHUNK, parts_ref.shape[0], CHUNK):
        total = total + parts_ref[start : start + CHUNK].astype(F32)
    total = total.astype(BF16)
    for start in range(0, out_ref.shape[0], CHUNK):
        out_ref[start : start + CHUNK] = total


def pair_kernel(own_ref, other_ref, *refs):
    out_ref = refs[-1]
    total = (own_ref[...].astype(F32) + other_ref[...].astype(F32)).astype(BF16)
    for start in range(0, out_ref.shape[0], CHUNK):
        out_ref[start : start + CHUNK] = total


def unpack_kernel(other, data_ref, *refs):
    sub_hbm, down_hbm, blocks, down, sems = refs[-5:]
    held = parity("gx") ^ other
    first = HALF // C
    rest = OFFSETS - first

    def widen(start, stop):
        rows = data_ref[start * C : stop * C].astype(F32)
        blocks[start:stop] = rows.reshape(stop - start, C, C)

    @pl.when(held == 0)
    def _():
        copies = []
        for k, (start, stop) in enumerate(((0, 6), (6, 12), (12, 17), (17, first))):
            widen(start, stop)
            copies.append(pltpu.make_async_copy(blocks.at[start:stop], sub_hbm.at[start:stop], sems.at[k]))
            copies[-1].start()
        for copy in copies:
            copy.wait()

    @pl.when(held == 1)
    def _():
        widen(0, rest)
        copies = [pltpu.make_async_copy(blocks.at[:rest], sub_hbm.at[first:], sems.at[0])]
        copies[0].start()
        for k, (start, stop) in enumerate(((0, 3), (3, 6), (6, 8))):
            for column in range(2):
                at = (rest + 8 * column + start) * C
                rows = data_ref[at : at + (stop - start) * C].astype(F32)
                down[start * C : stop * C, column * C : (column + 1) * C] = rows
            part = pl.ds(start * C, (stop - start) * C)
            copies.append(pltpu.make_async_copy(down.at[part], down_hbm.at[part], sems.at[k + 1]))
            copies[-1].start()
        for copy in copies:
            copy.wait()


def call(kernel, outs, scratch=(), flops=0, **options):
    return pl.pallas_call(
        kernel,
        out_shape=[jax.ShapeDtypeStruct(*out) for out in outs],
        scratch_shapes=list(scratch),
        cost_estimate=pl.CostEstimate(flops=flops, bytes_accessed=1 << 20, transcendentals=0),
        compiler_params=pltpu.CompilerParams(vmem_limit_bytes=40 * 1024 * 1024),
        **options,
    )


def reduce_all(own, send, after):
    rows, cols = lax.axis_size("gx"), lax.axis_size("gy")
    plane = [
        [i * cols + j for i in range(core, rows, 2) for j in (first, first + 1)]
        for core in range(2)
        for first in range(0, cols, 2)
    ]

    def trade(value, groups):
        return lax.all_to_all(value, AXES, 0, 0, axis_index_groups=groups, tiled=True)

    packed = ((HALF, C), BF16)
    (part,) = call(add_kernel, [packed])(own, swap(send, "gx", 0))
    (total,) = call(sum_kernel, [((CHUNK, C), BF16)])(trade(part, plane))
    for flip in (1, 2, 6):
        pairs = [(j, ((j >> 1) ^ flip) * 2 + (j & 1)) for j in range(cols)]
        copies = HALF if flip == 6 else CHUNK
        extra = (after,) if flip == 2 else ()
        (total,) = call(pair_kernel, [((copies, C), BF16)])(total, lax.ppermute(total, "gy", pairs), *extra)
    whole = trade(total, plane)
    return whole, swap(whole, "gx", 0)


def local(features, w_sub, w_down, cell_ids, send_rows, map_in, map_out, cotangent):
    ids = cell_ids[None]
    rows = features.shape[0]
    dense = ((CELLS, C), BF16)
    y_side = ((3 * LX * LZ, C), BF16)
    x_face_rows, x_ends = 3 * LY * LZ, 10 * LZ
    frame = (((LX + 2) * (LY + 2) * LZ, C), BF16)
    packed = ((HALF, C), BF16)
    framed = pltpu.VMEM((LX + 2, LY + 2, LZ, C), F32)

    place = ((CELLS, CELLS), BF16)
    from_corner, to_corner = call(places_kernel, [place, place], flops=LONG)()
    outs = [dense, dense, y_side, y_side, ((x_face_rows, C), BF16)]
    grid, hidden_grad, y_even, y_odd, x_odd = call(build_kernel, outs, flops=LONG)(
        from_corner, ids, features, cotangent, w_down
    )
    y_even, y_odd = swap_both(y_even, y_odd, "gy")
    x_odd = swap(x_odd, "gx", 1)
    outs = [((x_face_rows + x_ends, C), BF16), ((x_ends, C), BF16)]
    x_even, x_far = call(x_sides_kernel, outs, flops=LONG)(grid, hidden_grad, y_odd, y_even)
    x_even, x_far = swap_both(x_even, x_far, "gx")
    planes = (LX, LY + 4, LZ, C)
    early = call(
        early_kernel,
        [(planes, F32), ((LX, LY + 2, LZ, C), F32), ((LX + 2, LY + 2, LZ, C), F32), ((OFFSETS * C, C), F32)],
        flops=LONG,
    )(grid, hidden_grad, y_odd, y_even, w_sub)
    mid, taps = early[0], early[3]
    spread = ((2 * LY * LZ, 3 * C), BF16)
    send, grad, *kept = call(main_kernel, [packed, frame, spread, dense, (planes, F32)], flops=LONG)(
        to_corner, ids, *early, x_odd, x_far, x_even, cotangent, w_sub
    )
    spread, hidden, side = kept
    own, coarse = call(late_kernel, [packed, ((U_DEV, C2), BF16)], flops=LONG)(
        to_corner, mid, side, spread, hidden, cotangent, taps, w_down
    )
    feature_grad, done = call(feature_kernel, [((rows, C), BF16), ((16, C), BF16)], [framed], flops=LONG)(ids, grad, w_sub)
    whole, other = reduce_all(own, send, done)
    grads = [((OFFSETS, C, C), F32), ((8 * C, C2), F32)]
    scratch = [pltpu.VMEM((HALF // C, C, C), F32), pltpu.VMEM((8 * C, C2), F32), pltpu.SemaphoreType.DMA((4,))]
    in_hbm = [pl.BlockSpec(memory_space=pltpu.HBM)] * 2
    grads_own = call(functools.partial(unpack_kernel, 0), grads, scratch, LONG, out_specs=in_hbm)(whole)
    sub_grad, down_grad = call(
        functools.partial(unpack_kernel, 1),
        grads,
        scratch,
        in_specs=[pl.BlockSpec(memory_space=pltpu.VMEM), *in_hbm],
        out_specs=in_hbm,
        input_output_aliases={1: 0, 2: 1},
    )(other, *grads_own)
    return coarse, feature_grad, sub_grad, down_grad


def solution(mesh):
    rows = P(AXES, None)
    flat = P(AXES)
    maps = P(None, AXES)
    return jax.shard_map(
        local,
        mesh=mesh,
        in_specs=(rows, P(), P(), flat, flat, maps, maps, rows),
        out_specs=(rows, rows, P(), P()),
        check_vma=False,
    )
```

```python
import functools

import jax
import jax.numpy as jnp
from jax import lax
from jax.experimental import pallas as pl
from jax.experimental.pallas import tpu as pltpu
from jax.sharding import PartitionSpec as P

LX = 4
LY = 16
LZ = 8
CELLS = LX * LY * LZ
U_DEV = 64
C = 128
C2 = 256
OFFSETS = 27
AXES = ("gx", "gy")
PEERS = 32
CHUNK = 88
HALF = PEERS * CHUNK
LONG = 1 << 33

F32 = jnp.float32
BF16 = jnp.bfloat16


def swap_pairs(count):
    even = [(k, k ^ 1) for k in range(count)]
    odd = [(k, k + 1 if k % 2 else k - 1) for k in range(count)]
    return even, [(k, m) for k, m in odd if 0 <= m < count]


def swap(value, axis, kind):
    return lax.ppermute(value, axis, swap_pairs(lax.axis_size(axis))[kind])


def swap_both(first, second, axis):
    second = swap(second, axis, 1)
    return swap(first, axis, 0), second


def parity(axis):
    return lax.rem(lax.axis_index(axis), 2)


def pick(flag, when_zero, when_one):
    mask = jnp.full(when_zero.shape, flag, jnp.int32) == 0
    return jnp.where(mask, when_zero, when_one)


def dot(left, right, dims=((1,), (0,))):
    return lax.dot_general(left, right, (dims, ((), ())), preferred_element_type=F32)


def cell_onehot(ids):
    cells = lax.broadcasted_iota(jnp.int32, (CELLS, ids.shape[1]), 0)
    return jnp.where(cells == ids, 1.0, 0.0).astype(BF16)


def corner_onehot(row_axis):
    place = lax.broadcasted_iota(jnp.int32, (CELLS, CELLS), row_axis)
    cell = lax.broadcasted_iota(jnp.int32, (CELLS, CELLS), 1 - row_axis)
    corner, row = place >> 6, place & 63
    x = ((row >> 5) << 1) + (corner >> 2)
    y = (((row >> 2) & 7) << 1) + ((corner >> 1) & 1)
    z = ((row & 3) << 1) + (corner & 1)
    return jnp.where(((x * LY + y) * LZ + z) == cell, 1.0, 0.0).astype(BF16)


def shift_z(value, step):
    rows = value.shape[0]
    z = lax.broadcasted_iota(jnp.int32, value.shape, 0) & (LZ - 1)
    if step == 1:
        return jnp.where(z == 0, 0.0, pltpu.roll(value, 1, 0))
    return jnp.where(z == LZ - 1, 0.0, pltpu.roll(value, rows - 1, 0))


def y_sides(dense, hidden_grad):
    def face(near, edge):
        rows = [dense[:, near].reshape(2 * LX * LZ, C), hidden_grad[:, edge].reshape(LX * LZ, C)]
        return jnp.concatenate(rows, 0)

    return face(slice(0, 2), 0), face(slice(LY - 2, LY), LY - 1)


def split_y(rows):
    return rows[: 2 * LX * LZ].reshape(LX, 2 * LZ, C), rows[2 * LX * LZ :].reshape(LX, LZ, C)


def places_kernel(from_ref, to_ref):
    from_ref[...] = corner_onehot(1)
    to_ref[...] = corner_onehot(0)


def build_kernel(place_ref, ids, features, cot, w_down, grid_ref, hidden_ref, even_ref, odd_ref, x_odd_ref):
    onehot = cell_onehot(ids[...])
    dense = dot(onehot, features[...])
    active = dot(onehot, jnp.ones((onehot.shape[1], C), BF16)) > 0.5
    back_rows = dot(cot[...], w_down[...], ((1,), (1,))).astype(BF16)
    stacked = jnp.concatenate([back_rows[:, k * C : (k + 1) * C] for k in range(8)], 0)
    hidden_grad = jnp.where(active, dot(place_ref[...], stacked), 0.0)
    grid_ref[...] = dense.astype(BF16)
    hidden_ref[...] = hidden_grad.astype(BF16)
    low, high = y_sides(dense.reshape(LX, LY, LZ, C), hidden_grad.reshape(LX, LY, LZ, C))
    side = parity("gy")
    even_ref[...] = pick(side, high, low).astype(BF16)
    odd_ref[...] = pick(side, low, high).astype(BF16)
    first = x_face(dense, hidden_grad, 0)
    last = x_face(dense, hidden_grad, LX - 1)
    x_odd_ref[...] = pick(parity("gx"), first, last).astype(BF16)


def x_face(dense, hidden_grad, edge):
    plane = LY * LZ
    near = dense[: 2 * plane] if edge == 0 else dense[CELLS - 2 * plane :]
    return jnp.concatenate([near, hidden_grad[edge * plane : (edge + 1) * plane]], 0)


def y_halos(odd_ref, even_ref):
    even, odd = even_ref[...].astype(F32), odd_ref[...].astype(F32)
    side = parity("gy")
    return split_y(pick(side, odd, even)), split_y(pick(side, even, odd))


def x_sides_kernel(grid_ref, hidden_ref, y_odd_ref, y_even_ref, even_ref, odd_ref):
    (low, low_grad), (high, high_grad) = y_halos(y_odd_ref, y_even_ref)

    def corners(near, edge):
        rows = []
        for x in near:
            rows += [low[x], high[x]]
        return jnp.concatenate([*rows, low_grad[edge], high_grad[edge]], 0)

    first, last = corners((0, 1), 0), corners((LX - 2, LX - 1), LX - 1)
    dense, hidden_grad = grid_ref[...].astype(F32), hidden_ref[...].astype(F32)
    side = parity("gx")
    face = pick(side, x_face(dense, hidden_grad, LX - 1), x_face(dense, hidden_grad, 0))
    even_ref[...] = jnp.concatenate([face, pick(side, last, first)], 0).astype(BF16)
    odd_ref[...] = pick(side, first, last).astype(BF16)


def store_side(planes, rows):
    face, corner = 2 * LY * LZ, 3 * LY * LZ
    planes[:, 2 : LY + 2] = rows[:face].reshape(2, LY, LZ, C)
    ends = rows[corner : corner + 8 * LZ].reshape(2, 4, LZ, C)
    planes[:, 0:2] = ends[:, 0:2]
    planes[:, LY + 2 :] = ends[:, 2:4]
    grads = corner + 8 * LZ
    return jnp.concatenate([rows[grads : grads + LZ], rows[face:corner], rows[grads + LZ :]], 0)


def kernel_rows(w_sub, step_x):
    rows = []
    for step_y in range(3):
        first = step_x * 9 + step_y * 3
        rows.append(jnp.concatenate([w_sub[first + k] for k in range(3)], 1))
    return jnp.concatenate(rows, 0)


def frame_rows(planes):
    rows = planes.shape[0] * (LY + 2) * LZ
    return jnp.concatenate([planes[:, k : k + LY + 2].reshape(rows, C).astype(BF16) for k in range(3)], 1)


def fold(taps):
    return shift_z(taps[:, :C], 1) + taps[:, C : 2 * C] + shift_z(taps[:, 2 * C :], -1)


def unfold(grad):
    return jnp.concatenate([shift_z(grad, -1), grad, shift_z(grad, 1)], 1).astype(BF16)


def activate(pre_act, hidden_grad):
    sigmoid = 1.0 / (1.0 + jnp.exp(-pre_act))
    pre_grad = hidden_grad * sigmoid * (1.0 + pre_act * (1.0 - sigmoid))
    return pre_act * sigmoid, pre_grad.astype(BF16)


def inner_rows(value):
    return value[:, 1 : LY + 1].reshape(value.shape[0] * LY * LZ, C)


def early_kernel(grid_ref, hidden_ref, y_odd_ref, y_even_ref, w_sub, mid, hidden_mid, pre_ref, taps_ref):
    (low, low_grad), (high, high_grad) = y_halos(y_odd_ref, y_even_ref)
    mid[:, 0:2] = low.reshape(LX, 2, LZ, C)
    mid[:, LY + 2 :] = high.reshape(LX, 2, LZ, C)
    mid[:, 2 : LY + 2] = grid_ref[...].astype(F32).reshape(LX, LY, LZ, C)
    hidden_mid[:, 0] = low_grad
    hidden_mid[:, LY + 1] = high_grad
    hidden_mid[:, 1 : LY + 1] = hidden_ref[...].astype(F32).reshape(LX, LY, LZ, C)
    rows = frame_rows(mid[...])
    pre_ref[...] = jnp.zeros_like(pre_ref)
    for step_x in range(3):
        part = fold(dot(rows, kernel_rows(w_sub, step_x)))
        pre_ref[2 - step_x : 2 - step_x + LX] += part.reshape(LX, LY + 2, LZ, C)
    _, grad = activate(inner_rows(pre_ref[2:4]), inner_rows(hidden_mid[1:3]))
    spread = unfold(grad.astype(F32))
    for group in range(9):
        step_x, step_y = group // 3, group % 3
        window = mid[step_x : step_x + 2, step_y + 1 : step_y + 1 + LY].reshape(2 * LY * LZ, C)
        taps = dot(window.astype(BF16), spread, ((0,), (0,)))
        for k in range(3):
            taps_ref[(3 * group + k) * C : (3 * group + k + 1) * C] = taps[:, k * C : (k + 1) * C]


def store_half(half, out_ref, mid, side, spread_ref, hidden_ref, place_ref, cot, taps_ref):
    blocks = HALF // C

    def plane(x, step_y):
        source = side[x + 2 if x < 0 else x - 2] if x < 0 or x >= LX else mid[x]
        return source[step_y + 1 : step_y + 1 + LY].reshape(LY * LZ, C)

    for group in range(8) if half == 0 else (7, 8):
        step_x, step_y = group // 3, group % 3
        held = [k for k in range(3) if (3 * group + k) // blocks == half]
        window = jnp.concatenate([plane(step_x - 1, step_y), plane(LX + step_x - 2, step_y)], 0)
        spread = spread_ref[:, held[0] * C : (held[-1] + 1) * C]
        taps = dot(window.astype(BF16), spread, ((0,), (0,)))
        for k in held:
            block = 3 * group + k
            total = taps[:, (k - held[0]) * C : (k - held[0] + 1) * C] + taps_ref[block * C : (block + 1) * C]
            at = (block - half * blocks) * C
            out_ref[at : at + C] = total.astype(BF16)
    if half == 1:
        down = dot(coarse_rows(place_ref, hidden_ref), cot[...], ((0,), (0,))).astype(BF16)
        at = (OFFSETS - blocks) * C
        out_ref[at : at + 8 * C] = down[:, :C]
        out_ref[at + 8 * C : at + 16 * C] = down[:, C:]
        out_ref[at + 16 * C :] = jnp.zeros((HALF - at - 16 * C, C), BF16)


def coarse_rows(place_ref, hidden_ref):
    by_corner = dot(place_ref[...], hidden_ref[...]).astype(BF16)
    return jnp.concatenate([by_corner[k * U_DEV : (k + 1) * U_DEV] for k in range(8)], 1)


def store_of(other, out_ref, *refs):
    held = parity("gx") ^ other
    for half in range(2):
        pl.when(held == half)(functools.partial(store_half, half, out_ref, *refs))


def main_kernel(
    place_ref, ids_ref, mid, hidden_mid, pre_ref, taps_ref, x_odd_ref, x_ends_ref, x_even_ref, cot_ref, w_sub,
    send_ref, grad_ref, spread_ref, hidden_ref, side,
):
    x_odd = jnp.concatenate([x_odd_ref[...].astype(F32), x_ends_ref[...].astype(F32)], 0)
    x_even = x_even_ref[...].astype(F32)
    flag = parity("gx")
    low_grad = store_side(side.at[0:2], pick(flag, x_odd, x_even))
    high_grad = store_side(side.at[2:4], pick(flag, x_even, x_odd))
    column = (LY + 2) * LZ
    centre = kernel_rows(w_sub, 1)
    rows = frame_rows(side[0:2])
    outer = fold(dot(rows, kernel_rows(w_sub, 0)))
    first = pre_ref[0].reshape(column, C) + outer[:column] + fold(dot(rows[column:], centre))
    second = pre_ref[1].reshape(column, C) + outer[column:]
    rows = frame_rows(side[2:4])
    outer = fold(dot(rows, kernel_rows(w_sub, 2)))
    last = pre_ref[LX + 1].reshape(column, C) + outer[column:] + fold(dot(rows[:column], centre))
    before = pre_ref[LX].reshape(column, C) + outer[:column]
    pre_act = jnp.concatenate([first, second, pre_ref[2:LX].reshape(2 * column, C), before, last], 0)
    hidden_grad = jnp.concatenate([low_grad, hidden_mid[...].reshape(LX * column, C), high_grad], 0)
    hidden, pre_grad = activate(pre_act, hidden_grad)
    grad_ref[...] = pre_grad

    def framed(value):
        return value.reshape(LX + 2, LY + 2, LZ, C)

    grad = framed(pre_grad.astype(F32))
    spread_ref[...] = unfold(inner_rows(jnp.concatenate([grad[1:2], grad[LX : LX + 1]], 0)))
    active = dot(cell_onehot(ids_ref[...]), jnp.ones((ids_ref.shape[1], C), BF16)) > 0.5
    hidden_ref[...] = jnp.where(active, inner_rows(framed(hidden)[1 : LX + 1]), 0.0).astype(BF16)
    store_of(1, send_ref, mid, side, spread_ref, hidden_ref, place_ref, cot_ref, taps_ref)


def late_kernel(place_ref, mid, side, spread_ref, hidden_ref, cot_ref, taps_ref, w_down_ref, own_ref, coarse_ref):
    coarse_ref[...] = dot(coarse_rows(place_ref, hidden_ref), w_down_ref[...]).astype(BF16)
    store_of(0, own_ref, mid, side, spread_ref, hidden_ref, place_ref, cot_ref, taps_ref)


def feature_kernel(ids_ref, grad_ref, w_sub_ref, out_ref, done_ref, padded):
    done_ref[...] = jnp.zeros_like(done_ref)
    padded[...] = grad_ref[...].astype(F32).reshape(LX + 2, LY + 2, LZ, C)
    parts = [jnp.zeros((CELLS, C), F32)] * 3
    for step_x in range(3):
        for step_y in range(3):
            window = padded[2 - step_x : 2 - step_x + LX, 2 - step_y : 2 - step_y + LY]
            window = window.reshape(CELLS, C).astype(BF16)
            first = step_x * 9 + step_y * 3
            parts = [parts[k] + dot(window, w_sub_ref[first + k], ((1,), (1,))) for k in range(3)]
    total = shift_z(parts[0], -1) + parts[1] + shift_z(parts[2], 1)
    out_ref[...] = dot(cell_onehot(ids_ref[...]), total.astype(BF16), ((0,), (0,))).astype(BF16)


def add_kernel(own_ref, other_ref, out_ref):
    out_ref[...] = (own_ref[...].astype(F32) + other_ref[...].astype(F32)).astype(BF16)


def sum_kernel(parts_ref, out_ref):
    total = parts_ref[0].astype(F32)
    for k in range(1, PEERS):
        total = total + parts_ref[k].astype(F32)
    out_ref[...] = total.astype(BF16)


def pair_kernel(own_ref, other_ref, *refs):
    out_ref = refs[-1]
    total = (own_ref[...].astype(F32) + other_ref[...].astype(F32)).astype(BF16)
    if len(out_ref.shape) == 2:
        out_ref[...] = total
    else:
        for k in range(PEERS):
            out_ref[k] = total


def unpack_kernel(other, data_ref, *refs):
    sub_hbm, down_hbm, blocks, down, sems = refs[-5:]
    held = parity("gx") ^ other
    first = HALF // C
    rest = OFFSETS - first

    def widen(start, stop):
        rows = data_ref[start * C : stop * C].astype(F32)
        blocks[start:stop] = rows.reshape(stop - start, C, C)

    @pl.when(held == 0)
    def _():
        copies = []
        for k, (start, stop) in enumerate(((0, 6), (6, 12), (12, 17), (17, first))):
            widen(start, stop)
            copies.append(pltpu.make_async_copy(blocks.at[start:stop], sub_hbm.at[start:stop], sems.at[k]))
            copies[-1].start()
        for copy in copies:
            copy.wait()

    @pl.when(held == 1)
    def _():
        widen(0, rest)
        copies = [pltpu.make_async_copy(blocks.at[:rest], sub_hbm.at[first:], sems.at[0])]
        copies[0].start()
        for k, (start, stop) in enumerate(((0, 3), (3, 6), (6, 8))):
            for column in range(2):
                at = (rest + 8 * column + start) * C
                rows = data_ref[at : at + (stop - start) * C].astype(F32)
                down[start * C : stop * C, column * C : (column + 1) * C] = rows
            part = pl.ds(start * C, (stop - start) * C)
            copies.append(pltpu.make_async_copy(down.at[part], down_hbm.at[part], sems.at[k + 1]))
            copies[-1].start()
        for copy in copies:
            copy.wait()


def call(kernel, outs, scratch=(), flops=0, **options):
    return pl.pallas_call(
        kernel,
        out_shape=[jax.ShapeDtypeStruct(*out) for out in outs],
        scratch_shapes=list(scratch),
        cost_estimate=pl.CostEstimate(flops=flops, bytes_accessed=1 << 20, transcendentals=0),
        compiler_params=pltpu.CompilerParams(vmem_limit_bytes=40 * 1024 * 1024),
        **options,
    )


def reduce_all(own, send, after):
    rows, cols = lax.axis_size("gx"), lax.axis_size("gy")
    blocks = [
        [i * cols + j for i in range(core, rows, 2) for j in range(first, first + 4)]
        for core in range(2)
        for first in range(0, cols, 4)
    ]

    def trade(value):
        return lax.all_to_all(value, AXES, 0, 0, axis_index_groups=blocks, tiled=True)

    chunk = (CHUNK, C)
    (part,) = call(add_kernel, [((HALF, C), BF16)])(own, swap(send, "gx", 0))
    (total,) = call(sum_kernel, [(chunk, BF16)])(trade(part.reshape(PEERS, *chunk)))
    for flip, shape, extra in ((2, chunk, (after,)), (6, (PEERS, *chunk), ())):
        pairs = [(j, ((j >> 1) ^ flip) * 2 + (j & 1)) for j in range(cols)]
        (total,) = call(pair_kernel, [(shape, BF16)])(total, lax.ppermute(total, "gy", pairs), *extra)
    whole = trade(total).reshape(HALF, C)
    return whole, swap(whole, "gx", 0)


def local(features, w_sub, w_down, cell_ids, send_rows, map_in, map_out, cotangent):
    ids = cell_ids[None]
    rows = features.shape[0]
    dense = ((CELLS, C), BF16)
    y_side = ((3 * LX * LZ, C), BF16)
    x_face_rows, x_ends = 3 * LY * LZ, 10 * LZ
    frame = (((LX + 2) * (LY + 2) * LZ, C), BF16)
    packed = ((HALF, C), BF16)
    framed = pltpu.VMEM((LX + 2, LY + 2, LZ, C), F32)

    place = ((CELLS, CELLS), BF16)
    from_corner, to_corner = call(places_kernel, [place, place], flops=LONG)()
    outs = [dense, dense, y_side, y_side, ((x_face_rows, C), BF16)]
    grid, hidden_grad, y_even, y_odd, x_odd = call(build_kernel, outs, flops=LONG)(
        from_corner, ids, features, cotangent, w_down
    )
    y_even, y_odd = swap_both(y_even, y_odd, "gy")
    x_odd = swap(x_odd, "gx", 1)
    outs = [((x_face_rows + x_ends, C), BF16), ((x_ends, C), BF16)]
    x_even, x_far = call(x_sides_kernel, outs, flops=LONG)(grid, hidden_grad, y_odd, y_even)
    x_even, x_far = swap_both(x_even, x_far, "gx")
    planes = (LX, LY + 4, LZ, C)
    early = call(
        early_kernel,
        [(planes, F32), ((LX, LY + 2, LZ, C), F32), ((LX + 2, LY + 2, LZ, C), F32), ((OFFSETS * C, C), F32)],
        flops=LONG,
    )(grid, hidden_grad, y_odd, y_even, w_sub)
    mid, taps = early[0], early[3]
    spread = ((2 * LY * LZ, 3 * C), BF16)
    send, grad, *kept = call(main_kernel, [packed, frame, spread, dense, (planes, F32)], flops=LONG)(
        to_corner, ids, *early, x_odd, x_far, x_even, cotangent, w_sub
    )
    spread, hidden, side = kept
    own, coarse = call(late_kernel, [packed, ((U_DEV, C2), BF16)], flops=LONG)(
        to_corner, mid, side, spread, hidden, cotangent, taps, w_down
    )
    feature_grad, done = call(feature_kernel, [((rows, C), BF16), ((16, C), BF16)], [framed], flops=LONG)(ids, grad, w_sub)
    whole, other = reduce_all(own, send, done)
    grads = [((OFFSETS, C, C), F32), ((8 * C, C2), F32)]
    scratch = [pltpu.VMEM((HALF // C, C, C), F32), pltpu.VMEM((8 * C, C2), F32), pltpu.SemaphoreType.DMA((4,))]
    in_hbm = [pl.BlockSpec(memory_space=pltpu.HBM)] * 2
    grads_own = call(functools.partial(unpack_kernel, 0), grads, scratch, LONG, out_specs=in_hbm)(whole)
    sub_grad, down_grad = call(
        functools.partial(unpack_kernel, 1),
        grads,
        scratch,
        in_specs=[pl.BlockSpec(memory_space=pltpu.VMEM), *in_hbm],
        out_specs=in_hbm,
        input_output_aliases={1: 0, 2: 1},
    )(other, *grads_own)
    return coarse, feature_grad, sub_grad, down_grad


def solution(mesh):
    rows = P(AXES, None)
    flat = P(AXES)
    maps = P(None, AXES)
    return jax.shard_map(
        local,
        mesh=mesh,
        in_specs=(rows, P(), P(), flat, flat, maps, maps, rows),
        out_specs=(rows, rows, P(), P()),
        check_vma=False,
    )
```

```python
import functools

import jax
import jax.numpy as jnp
from jax import lax
from jax.experimental import pallas as pl
from jax.experimental.pallas import tpu as pltpu
from jax.sharding import PartitionSpec as P

LX = 4
LY = 16
LZ = 8
CELLS = LX * LY * LZ
U_DEV = 64
C = 128
C2 = 256
OFFSETS = 27
AXES = ("gx", "gy")
PEERS = 32
CHUNK = 88
HALF = PEERS * CHUNK
LONG = 1 << 33

F32 = jnp.float32
BF16 = jnp.bfloat16


def swap_pairs(count):
    even = [(k, k ^ 1) for k in range(count)]
    odd = [(k, k + 1 if k % 2 else k - 1) for k in range(count)]
    return even, [(k, m) for k, m in odd if 0 <= m < count]


def swap(value, axis, kind):
    return lax.ppermute(value, axis, swap_pairs(lax.axis_size(axis))[kind])


def swap_both(first, second, axis):
    second = swap(second, axis, 1)
    return swap(first, axis, 0), second


def parity(axis):
    return lax.rem(lax.axis_index(axis), 2)


def pick(flag, when_zero, when_one):
    mask = jnp.full(when_zero.shape, flag, jnp.int32) == 0
    return jnp.where(mask, when_zero, when_one)


def dot(left, right, dims=((1,), (0,))):
    return lax.dot_general(left, right, (dims, ((), ())), preferred_element_type=F32)


def cell_onehot(ids):
    cells = lax.broadcasted_iota(jnp.int32, (CELLS, ids.shape[1]), 0)
    return jnp.where(cells == ids, 1.0, 0.0).astype(BF16)


def corner_onehot(row_axis):
    place = lax.broadcasted_iota(jnp.int32, (CELLS, CELLS), row_axis)
    cell = lax.broadcasted_iota(jnp.int32, (CELLS, CELLS), 1 - row_axis)
    corner, row = place >> 6, place & 63
    x = ((row >> 5) << 1) + (corner >> 2)
    y = (((row >> 2) & 7) << 1) + ((corner >> 1) & 1)
    z = ((row & 3) << 1) + (corner & 1)
    return jnp.where(((x * LY + y) * LZ + z) == cell, 1.0, 0.0).astype(BF16)


def shift_z(value, step):
    rows = value.shape[0]
    z = lax.broadcasted_iota(jnp.int32, value.shape, 0) & (LZ - 1)
    if step == 1:
        return jnp.where(z == 0, 0.0, pltpu.roll(value, 1, 0))
    return jnp.where(z == LZ - 1, 0.0, pltpu.roll(value, rows - 1, 0))


def y_sides(dense, hidden_grad):
    def face(near, edge):
        rows = [dense[:, near].reshape(2 * LX * LZ, C), hidden_grad[:, edge].reshape(LX * LZ, C)]
        return jnp.concatenate(rows, 0)

    return face(slice(0, 2), 0), face(slice(LY - 2, LY), LY - 1)


def split_y(rows):
    return rows[: 2 * LX * LZ].reshape(LX, 2 * LZ, C), rows[2 * LX * LZ :].reshape(LX, LZ, C)


def places_kernel(from_ref, to_ref):
    from_ref[...] = corner_onehot(1)
    to_ref[...] = corner_onehot(0)


def build_kernel(place_ref, ids, features, cot, w_down, grid_ref, hidden_ref, even_ref, odd_ref, x_odd_ref):
    onehot = cell_onehot(ids[...])
    both = dot(onehot, jnp.concatenate([features[...], jnp.ones((onehot.shape[1], C), BF16)], 1))
    dense, active = both[:, :C], both[:, C:] > 0.5
    back_rows = dot(cot[...], w_down[...], ((1,), (1,))).astype(BF16)
    stacked = jnp.concatenate([back_rows[:, k * C : (k + 1) * C] for k in range(8)], 0)
    hidden_grad = jnp.where(active, dot(place_ref[...], stacked), 0.0)
    grid_ref[...] = dense.astype(BF16)
    hidden_ref[...] = hidden_grad.astype(BF16)
    low, high = y_sides(dense.reshape(LX, LY, LZ, C), hidden_grad.reshape(LX, LY, LZ, C))
    side = parity("gy")
    even_ref[...] = pick(side, high, low).astype(BF16)
    odd_ref[...] = pick(side, low, high).astype(BF16)
    first = x_face(dense, hidden_grad, 0)
    last = x_face(dense, hidden_grad, LX - 1)
    x_odd_ref[...] = pick(parity("gx"), first, last).astype(BF16)


def x_face(dense, hidden_grad, edge):
    plane = LY * LZ
    near = dense[: 2 * plane] if edge == 0 else dense[CELLS - 2 * plane :]
    return jnp.concatenate([near, hidden_grad[edge * plane : (edge + 1) * plane]], 0)


def y_halos(odd_ref, even_ref):
    even, odd = even_ref[...].astype(F32), odd_ref[...].astype(F32)
    side = parity("gy")
    return split_y(pick(side, odd, even)), split_y(pick(side, even, odd))


def x_sides_kernel(grid_ref, hidden_ref, y_odd_ref, y_even_ref, even_ref, odd_ref):
    (low, low_grad), (high, high_grad) = y_halos(y_odd_ref, y_even_ref)

    def corners(near, edge):
        rows = []
        for x in near:
            rows += [low[x], high[x]]
        return jnp.concatenate([*rows, low_grad[edge], high_grad[edge]], 0)

    first, last = corners((0, 1), 0), corners((LX - 2, LX - 1), LX - 1)
    dense, hidden_grad = grid_ref[...].astype(F32), hidden_ref[...].astype(F32)
    side = parity("gx")
    face = pick(side, x_face(dense, hidden_grad, LX - 1), x_face(dense, hidden_grad, 0))
    even_ref[...] = jnp.concatenate([face, pick(side, last, first)], 0).astype(BF16)
    odd_ref[...] = pick(side, first, last).astype(BF16)


def store_side(planes, rows):
    face, corner = 2 * LY * LZ, 3 * LY * LZ
    planes[:, 2 : LY + 2] = rows[:face].reshape(2, LY, LZ, C)
    ends = rows[corner : corner + 8 * LZ].reshape(2, 4, LZ, C)
    planes[:, 0:2] = ends[:, 0:2]
    planes[:, LY + 2 :] = ends[:, 2:4]
    grads = corner + 8 * LZ
    return jnp.concatenate([rows[grads : grads + LZ], rows[face:corner], rows[grads + LZ :]], 0)


def kernel_rows(w_sub, step_x):
    rows = []
    for step_y in range(3):
        first = step_x * 9 + step_y * 3
        rows.append(jnp.concatenate([w_sub[first + k] for k in range(3)], 1))
    return jnp.concatenate(rows, 0)


def frame_rows(planes):
    rows = planes.shape[0] * (LY + 2) * LZ
    return jnp.concatenate([planes[:, k : k + LY + 2].reshape(rows, C).astype(BF16) for k in range(3)], 1)


def inner_windows(planes):
    rows = planes.shape[0] * LY * LZ
    return jnp.concatenate([planes[:, k + 1 : k + 1 + LY].reshape(rows, C).astype(BF16) for k in range(3)], 1)


def fold(taps):
    return shift_z(taps[:, :C], 1) + taps[:, C : 2 * C] + shift_z(taps[:, 2 * C :], -1)


def unfold(grad):
    return jnp.concatenate([shift_z(grad, -1), grad, shift_z(grad, 1)], 1).astype(BF16)


def activate(pre_act, hidden_grad):
    sigmoid = 1.0 / (1.0 + jnp.exp(-pre_act))
    pre_grad = hidden_grad * sigmoid * (1.0 + pre_act * (1.0 - sigmoid))
    return pre_act * sigmoid, pre_grad.astype(BF16)


def inner_rows(value):
    return value[:, 1 : LY + 1].reshape(value.shape[0] * LY * LZ, C)


def early_kernel(grid_ref, hidden_ref, y_odd_ref, y_even_ref, w_sub, mid, hidden_mid, pre_ref, taps_ref, inner_ref):
    (low, low_grad), (high, high_grad) = y_halos(y_odd_ref, y_even_ref)
    mid[:, 0:2] = low.reshape(LX, 2, LZ, C)
    mid[:, LY + 2 :] = high.reshape(LX, 2, LZ, C)
    mid[:, 2 : LY + 2] = grid_ref[...].astype(F32).reshape(LX, LY, LZ, C)
    hidden_mid[:, 0] = low_grad
    hidden_mid[:, LY + 1] = high_grad
    hidden_mid[:, 1 : LY + 1] = hidden_ref[...].astype(F32).reshape(LX, LY, LZ, C)
    rows = frame_rows(mid[...])
    pre_ref[...] = jnp.zeros_like(pre_ref)
    for step_x in range(3):
        part = fold(dot(rows, kernel_rows(w_sub, step_x)))
        pre_ref[2 - step_x : 2 - step_x + LX] += part.reshape(LX, LY + 2, LZ, C)
    inner_ref[...], grad = activate(inner_rows(pre_ref[2:4]), inner_rows(hidden_mid[1:3]))
    spread = unfold(grad.astype(F32))
    for group in range(9):
        step_x, step_y = group // 3, group % 3
        window = mid[step_x : step_x + 2, step_y + 1 : step_y + 1 + LY].reshape(2 * LY * LZ, C)
        taps = dot(window.astype(BF16), spread, ((0,), (0,)))
        for k in range(3):
            taps_ref[(3 * group + k) * C : (3 * group + k + 1) * C] = taps[:, k * C : (k + 1) * C]


def store_half(half, out_ref, mid, side, spread_ref, hidden_ref, place_ref, cot, taps_ref):
    blocks = HALF // C

    def plane(x, step_y):
        source = side[x + 2 if x < 0 else x - 2] if x < 0 or x >= LX else mid[x]
        return source[step_y + 1 : step_y + 1 + LY].reshape(LY * LZ, C)

    for group in range(8) if half == 0 else (7, 8):
        step_x, step_y = group // 3, group % 3
        held = [k for k in range(3) if (3 * group + k) // blocks == half]
        window = jnp.concatenate([plane(step_x - 1, step_y), plane(LX + step_x - 2, step_y)], 0)
        spread = spread_ref[:, held[0] * C : (held[-1] + 1) * C]
        taps = dot(window.astype(BF16), spread, ((0,), (0,)))
        for k in held:
            block = 3 * group + k
            total = taps[:, (k - held[0]) * C : (k - held[0] + 1) * C] + taps_ref[block * C : (block + 1) * C]
            at = (block - half * blocks) * C
            out_ref[at : at + C] = total.astype(BF16)
    if half == 1:
        down = dot(coarse_rows(place_ref, hidden_ref), cot[...], ((0,), (0,))).astype(BF16)
        at = (OFFSETS - blocks) * C
        out_ref[at : at + 8 * C] = down[:, :C]
        out_ref[at + 8 * C : at + 16 * C] = down[:, C:]
        out_ref[at + 16 * C :] = jnp.zeros((HALF - at - 16 * C, C), BF16)


def coarse_rows(place_ref, hidden_ref):
    by_corner = dot(place_ref[...], hidden_ref[...]).astype(BF16)
    return jnp.concatenate([by_corner[k * U_DEV : (k + 1) * U_DEV] for k in range(8)], 1)


def store_of(other, out_ref, *refs):
    held = parity("gx") ^ other
    for half in range(2):
        pl.when(held == half)(functools.partial(store_half, half, out_ref, *refs))


def main_kernel(
    place_ref, ids_ref, mid, hidden_mid, pre_ref, taps_ref, inner_ref, x_odd_ref, x_ends_ref, x_even_ref, cot_ref, w_sub,
    send_ref, spread_ref, hidden_ref, side, side_grad,
):
    x_odd = jnp.concatenate([x_odd_ref[...].astype(F32), x_ends_ref[...].astype(F32)], 0)
    x_even = x_even_ref[...].astype(F32)
    flag = parity("gx")
    side_grad[0] = store_side(side.at[0:2], pick(flag, x_odd, x_even))
    side_grad[1] = store_side(side.at[2:4], pick(flag, x_even, x_odd))
    plane = LY * LZ
    rows = inner_windows(side[1:3])
    first = inner_rows(pre_ref[1:2]) + fold(dot(rows[:plane], kernel_rows(w_sub, 0)))
    last = inner_rows(pre_ref[LX : LX + 1]) + fold(dot(rows[plane:], kernel_rows(w_sub, 2)))
    hidden_grad = [inner_rows(hidden_mid[0:1]), inner_rows(hidden_mid[LX - 1 : LX])]
    outer, grad = activate(jnp.concatenate([first, last], 0), jnp.concatenate(hidden_grad, 0))
    spread_ref[...] = unfold(grad.astype(F32))
    active = dot(cell_onehot(ids_ref[...]), jnp.ones((ids_ref.shape[1], C), BF16)) > 0.5
    hidden = jnp.concatenate([outer[:plane], inner_ref[...], outer[plane:]], 0)
    hidden_ref[...] = jnp.where(active, hidden, 0.0).astype(BF16)
    store_of(1, send_ref, mid, side, spread_ref, hidden_ref, place_ref, cot_ref, taps_ref)


def late_kernel(place_ref, mid, side, spread_ref, hidden_ref, cot_ref, taps_ref, w_down_ref, own_ref, coarse_ref):
    coarse_ref[...] = dot(coarse_rows(place_ref, hidden_ref), w_down_ref[...]).astype(BF16)
    store_of(0, own_ref, mid, side, spread_ref, hidden_ref, place_ref, cot_ref, taps_ref)


def feature_kernel(ids_ref, side, side_grad, hidden_mid, pre_ref, w_sub_ref, after_ref, out_ref, done_ref, padded):
    done_ref[...] = jnp.zeros_like(done_ref)
    column = (LY + 2) * LZ
    centre = kernel_rows(w_sub_ref, 1)
    rows = frame_rows(side[0:2])
    outer = fold(dot(rows, kernel_rows(w_sub_ref, 0)))
    first = pre_ref[0].reshape(column, C) + outer[:column] + fold(dot(rows[column:], centre))
    second = pre_ref[1].reshape(column, C) + outer[column:]
    rows = frame_rows(side[2:4])
    outer = fold(dot(rows, kernel_rows(w_sub_ref, 2)))
    last = pre_ref[LX + 1].reshape(column, C) + outer[column:] + fold(dot(rows[:column], centre))
    before = pre_ref[LX].reshape(column, C) + outer[:column]
    pre_act = jnp.concatenate([first, second, pre_ref[2:LX].reshape(2 * column, C), before, last], 0)
    hidden_grad = jnp.concatenate([side_grad[0], hidden_mid[...].reshape(LX * column, C), side_grad[1]], 0)
    _, pre_grad = activate(pre_act, hidden_grad)
    padded[...] = pre_grad.astype(F32).reshape(LX + 2, LY + 2, LZ, C)
    parts = [jnp.zeros((CELLS, C), F32)] * 3
    for step_x in range(3):
        for step_y in range(3):
            window = padded[2 - step_x : 2 - step_x + LX, 2 - step_y : 2 - step_y + LY]
            window = window.reshape(CELLS, C).astype(BF16)
            first = step_x * 9 + step_y * 3
            parts = [parts[k] + dot(window, w_sub_ref[first + k], ((1,), (1,))) for k in range(3)]
    total = shift_z(parts[0], -1) + parts[1] + shift_z(parts[2], 1)
    out_ref[...] = dot(cell_onehot(ids_ref[...]), total.astype(BF16), ((0,), (0,))).astype(BF16)


def add_kernel(own_ref, other_ref, out_ref):
    out_ref[...] = (own_ref[...].astype(F32) + other_ref[...].astype(F32)).astype(BF16)


def sum_kernel(parts_ref, out_ref):
    total = parts_ref[0].astype(F32)
    for k in range(1, PEERS):
        total = total + parts_ref[k].astype(F32)
    out_ref[...] = total.astype(BF16)


def pair_kernel(own_ref, other_ref, *refs):
    out_ref = refs[-1]
    total = (own_ref[...].astype(F32) + other_ref[...].astype(F32)).astype(BF16)
    if len(out_ref.shape) == 2:
        out_ref[...] = total
    else:
        for k in range(PEERS):
            out_ref[k] = total


def unpack_kernel(other, data_ref, *refs):
    sub_hbm, down_hbm, blocks, down, sems = refs[-5:]
    held = parity("gx") ^ other
    first = HALF // C
    rest = OFFSETS - first

    def widen(start, stop):
        rows = data_ref[start * C : stop * C].astype(F32)
        blocks[start:stop] = rows.reshape(stop - start, C, C)

    @pl.when(held == 0)
    def _():
        copies = []
        for k, (start, stop) in enumerate(((0, 6), (6, 12), (12, 17), (17, first))):
            widen(start, stop)
            copies.append(pltpu.make_async_copy(blocks.at[start:stop], sub_hbm.at[start:stop], sems.at[k]))
            copies[-1].start()
        for copy in copies:
            copy.wait()

    @pl.when(held == 1)
    def _():
        widen(0, rest)
        copies = [pltpu.make_async_copy(blocks.at[:rest], sub_hbm.at[first:], sems.at[0])]
        copies[0].start()
        for k, (start, stop) in enumerate(((0, 3), (3, 6), (6, 8))):
            for column in range(2):
                at = (rest + 8 * column + start) * C
                rows = data_ref[at : at + (stop - start) * C].astype(F32)
                down[start * C : stop * C, column * C : (column + 1) * C] = rows
            part = pl.ds(start * C, (stop - start) * C)
            copies.append(pltpu.make_async_copy(down.at[part], down_hbm.at[part], sems.at[k + 1]))
            copies[-1].start()
        for copy in copies:
            copy.wait()


def call(kernel, outs, scratch=(), flops=0, **options):
    return pl.pallas_call(
        kernel,
        out_shape=[jax.ShapeDtypeStruct(*out) for out in outs],
        scratch_shapes=list(scratch),
        cost_estimate=pl.CostEstimate(flops=flops, bytes_accessed=1 << 20, transcendentals=0),
        compiler_params=pltpu.CompilerParams(vmem_limit_bytes=40 * 1024 * 1024),
        **options,
    )


def reduce_all(own, send, beside):
    rows, cols = lax.axis_size("gx"), lax.axis_size("gy")
    blocks = [
        [i * cols + j for i in range(core, rows, 2) for j in range(first, first + 4)]
        for core in range(2)
        for first in range(0, cols, 4)
    ]

    def trade(value):
        return lax.all_to_all(value, AXES, 0, 0, axis_index_groups=blocks, tiled=True)

    chunk = (CHUNK, C)
    (part,) = call(add_kernel, [((HALF, C), BF16)])(own, swap(send, "gx", 0))
    (total,) = call(sum_kernel, [(chunk, BF16)])(trade(part.reshape(PEERS, *chunk)))
    for flip, shape in ((2, chunk), (6, (PEERS, *chunk))):
        pairs = [(j, ((j >> 1) ^ flip) * 2 + (j & 1)) for j in range(cols)]
        arrived = lax.ppermute(total, "gy", pairs)
        extra = ()
        if flip == 6:
            result, mark = beside(total)
            extra = (mark,)
        (total,) = call(pair_kernel, [(shape, BF16)])(total, arrived, *extra)
    whole = trade(total).reshape(HALF, C)
    return result, whole, swap(whole, "gx", 0)


def local(features, w_sub, w_down, cell_ids, send_rows, map_in, map_out, cotangent):
    ids = cell_ids[None]
    rows = features.shape[0]
    dense = ((CELLS, C), BF16)
    y_side = ((3 * LX * LZ, C), BF16)
    x_face_rows, x_ends = 3 * LY * LZ, 10 * LZ
    packed = ((HALF, C), BF16)
    framed = pltpu.VMEM((LX + 2, LY + 2, LZ, C), F32)

    place = ((CELLS, CELLS), BF16)
    from_corner, to_corner = call(places_kernel, [place, place], flops=LONG)()
    outs = [dense, dense, y_side, y_side, ((x_face_rows, C), BF16)]
    grid, hidden_grad, y_even, y_odd, x_odd = call(build_kernel, outs, flops=LONG)(
        from_corner, ids, features, cotangent, w_down
    )
    y_even, y_odd = swap_both(y_even, y_odd, "gy")
    x_odd = swap(x_odd, "gx", 1)
    outs = [((x_face_rows + x_ends, C), BF16), ((x_ends, C), BF16)]
    x_even, x_far = call(x_sides_kernel, outs, flops=LONG)(grid, hidden_grad, y_odd, y_even)
    x_even, x_far = swap_both(x_even, x_far, "gx")
    planes = (LX, LY + 4, LZ, C)
    inner = (2 * LY * LZ, C)
    early = call(
        early_kernel,
        [(planes, F32), ((LX, LY + 2, LZ, C), F32), ((LX + 2, LY + 2, LZ, C), F32), ((OFFSETS * C, C), F32), (inner, F32)],
        flops=LONG,
    )(grid, hidden_grad, y_odd, y_even, w_sub)
    mid, hidden_mid, pre_act, taps, _ = early
    outs = [packed, ((2 * LY * LZ, 3 * C), BF16), dense, (planes, F32), ((2, (LY + 2) * LZ, C), F32)]
    send, spread, hidden, side, side_grad = call(main_kernel, outs, flops=LONG)(
        to_corner, ids, *early, x_odd, x_far, x_even, cotangent, w_sub
    )
    own, coarse = call(late_kernel, [packed, ((U_DEV, C2), BF16)], flops=LONG)(
        to_corner, mid, side, spread, hidden, cotangent, taps, w_down
    )

    def beside(value):
        outs = [((rows, C), BF16), ((16, C), BF16)]
        return call(feature_kernel, outs, [framed], flops=LONG)(
            ids, side, side_grad, hidden_mid, pre_act, w_sub, value
        )

    feature_grad, whole, other = reduce_all(own, send, beside)
    grads = [((OFFSETS, C, C), F32), ((8 * C, C2), F32)]
    scratch = [pltpu.VMEM((HALF // C, C, C), F32), pltpu.VMEM((8 * C, C2), F32), pltpu.SemaphoreType.DMA((4,))]
    in_hbm = [pl.BlockSpec(memory_space=pltpu.HBM)] * 2
    grads_own = call(functools.partial(unpack_kernel, 0), grads, scratch, LONG, out_specs=in_hbm)(whole)
    sub_grad, down_grad = call(
        functools.partial(unpack_kernel, 1),
        grads,
        scratch,
        in_specs=[pl.BlockSpec(memory_space=pltpu.VMEM), *in_hbm],
        out_specs=in_hbm,
        input_output_aliases={1: 0, 2: 1},
    )(other, *grads_own)
    return coarse, feature_grad, sub_grad, down_grad


def solution(mesh):
    rows = P(AXES, None)
    flat = P(AXES)
    maps = P(None, AXES)
    return jax.shard_map(
        local,
        mesh=mesh,
        in_specs=(rows, P(), P(), flat, flat, maps, maps, rows),
        out_specs=(rows, rows, P(), P()),
        check_vma=False,
    )
```

```python
import functools

import jax
import jax.numpy as jnp
from jax import lax
from jax.experimental import pallas as pl
from jax.experimental.pallas import tpu as pltpu
from jax.sharding import PartitionSpec as P

LX = 4
LY = 16
LZ = 8
CELLS = LX * LY * LZ
U_DEV = 64
C = 128
C2 = 256
OFFSETS = 27
AXES = ("gx", "gy")
PEERS = 32
CHUNK = 88
HALF = PEERS * CHUNK
LONG = 1 << 33

F32 = jnp.float32
BF16 = jnp.bfloat16


def swap_pairs(count):
    even = [(k, k ^ 1) for k in range(count)]
    odd = [(k, k + 1 if k % 2 else k - 1) for k in range(count)]
    return even, [(k, m) for k, m in odd if 0 <= m < count]


def swap(value, axis, kind):
    return lax.ppermute(value, axis, swap_pairs(lax.axis_size(axis))[kind])


def swap_both(first, second, axis):
    second = swap(second, axis, 1)
    return swap(first, axis, 0), second


def parity(axis):
    return lax.rem(lax.axis_index(axis), 2)


def pick(flag, when_zero, when_one):
    mask = jnp.full(when_zero.shape, flag, jnp.int32) == 0
    return jnp.where(mask, when_zero, when_one)


def dot(left, right, dims=((1,), (0,))):
    return lax.dot_general(left, right, (dims, ((), ())), preferred_element_type=F32)


def cell_onehot(ids):
    cells = lax.broadcasted_iota(jnp.int32, (CELLS, ids.shape[1]), 0)
    return jnp.where(cells == ids, 1.0, 0.0).astype(BF16)


def corner_onehot(row_axis):
    place = lax.broadcasted_iota(jnp.int32, (CELLS, CELLS), row_axis)
    cell = lax.broadcasted_iota(jnp.int32, (CELLS, CELLS), 1 - row_axis)
    corner, row = place >> 6, place & 63
    x = ((row >> 5) << 1) + (corner >> 2)
    y = (((row >> 2) & 7) << 1) + ((corner >> 1) & 1)
    z = ((row & 3) << 1) + (corner & 1)
    return jnp.where(((x * LY + y) * LZ + z) == cell, 1.0, 0.0).astype(BF16)


def shift_z(value, step):
    rows = value.shape[0]
    z = lax.broadcasted_iota(jnp.int32, value.shape, 0) & (LZ - 1)
    if step == 1:
        return jnp.where(z == 0, 0.0, pltpu.roll(value, 1, 0))
    return jnp.where(z == LZ - 1, 0.0, pltpu.roll(value, rows - 1, 0))


def y_sides(dense, active, cot):
    def face(near, edge):
        first = edge // 2 * (LZ // 2)
        coarse = [cot[k * 32 + first : k * 32 + first + LZ // 2] for k in range(2)]
        coarse = jnp.concatenate(coarse, 0)
        rows = [dense[:, near].reshape(2 * LX * LZ, C), active[:, edge].reshape(LX * LZ, C)]
        return jnp.concatenate([*rows, coarse[:, :C], coarse[:, C:]], 0)

    return face(slice(0, 2), 0), face(slice(LY - 2, LY), LY - 1)


def split_y(rows):
    feature, mask = 2 * LX * LZ, 3 * LX * LZ
    cot = jnp.concatenate([rows[mask : mask + LZ], rows[mask + LZ :]], 1)
    return rows[:feature].reshape(LX, 2 * LZ, C), rows[feature:mask].reshape(LX, LZ, C), cot


def places_kernel(from_ref, to_ref):
    from_ref[...] = corner_onehot(1)
    to_ref[...] = corner_onehot(0)


def place_rows(ids, features):
    onehot = cell_onehot(ids)
    both = dot(onehot, jnp.concatenate([features, jnp.ones(features.shape, BF16)], 1))
    return both[:, :C], both[:, C:]


def build_kernel(place_ref, ids, features, cot, grid_ref, active_ref, even_ref, odd_ref):
    dense, active = place_rows(ids[...], features[...])
    grid_ref[...] = dense.astype(BF16)
    active_ref[...] = active.astype(BF16)
    shape = (LX, LY, LZ, C)
    low, high = y_sides(dense.reshape(shape), active.reshape(shape), cot[...].astype(F32))
    side = parity("gy")
    even_ref[...] = pick(side, high, low).astype(BF16)
    odd_ref[...] = pick(side, low, high).astype(BF16)


def back_kernel(place_ref, grid_ref, active_ref, cot, w_down, hidden_ref, x_odd_ref):
    back_rows = dot(cot[...], w_down[...], ((1,), (1,))).astype(BF16)
    stacked = jnp.concatenate([back_rows[:, k * C : (k + 1) * C] for k in range(8)], 0)
    hidden_grad = jnp.where(active_ref[...].astype(F32) > 0.5, dot(place_ref[...], stacked), 0.0)
    hidden_ref[...] = hidden_grad.astype(BF16)
    dense = grid_ref[...].astype(F32)
    first = x_face(dense, hidden_grad, 0)
    last = x_face(dense, hidden_grad, LX - 1)
    x_odd_ref[...] = pick(parity("gx"), first, last).astype(BF16)


def x_face(dense, hidden_grad, edge):
    plane = LY * LZ
    near = dense[: 2 * plane] if edge == 0 else dense[CELLS - 2 * plane :]
    return jnp.concatenate([near, hidden_grad[edge * plane : (edge + 1) * plane]], 0)


def y_halos(odd_ref, even_ref):
    even, odd = even_ref[...].astype(F32), odd_ref[...].astype(F32)
    side = parity("gy")
    return split_y(pick(side, odd, even)), split_y(pick(side, even, odd))


def x_sides_kernel(grid_ref, hidden_ref, y_odd_ref, y_even_ref, even_ref, odd_ref):
    (low, low_mask, low_cot), (high, high_mask, high_cot) = y_halos(y_odd_ref, y_even_ref)

    def corners(near, edge):
        rows = []
        for x in near:
            rows += [low[x], high[x]]
        at = edge // 2 * (LZ // 2)
        coarse = jnp.concatenate([low_cot[at : at + LZ // 2], high_cot[at : at + LZ // 2]], 0)
        return jnp.concatenate([*rows, low_mask[edge], high_mask[edge], coarse[:, :C], coarse[:, C:]], 0)

    first, last = corners((0, 1), 0), corners((LX - 2, LX - 1), LX - 1)
    dense, hidden_grad = grid_ref[...].astype(F32), hidden_ref[...].astype(F32)
    side = parity("gx")
    face = pick(side, x_face(dense, hidden_grad, LX - 1), x_face(dense, hidden_grad, 0))
    even_ref[...] = jnp.concatenate([face, pick(side, last, first)], 0).astype(BF16)
    odd_ref[...] = pick(side, first, last).astype(BF16)


def store_side(planes, rows):
    face, corner = 2 * LY * LZ, 3 * LY * LZ
    planes[:, 2 : LY + 2] = rows[:face].reshape(2, LY, LZ, C)
    ends = rows[corner : corner + 8 * LZ].reshape(2, 4, LZ, C)
    planes[:, 0:2] = ends[:, 0:2]
    planes[:, LY + 2 :] = ends[:, 2:4]
    grads = corner + 8 * LZ
    return jnp.concatenate([rows[grads : grads + LZ], rows[face:corner], rows[grads + LZ : grads + 2 * LZ]], 0)


def kernel_rows(w_sub, step_x):
    rows = []
    for step_y in range(3):
        first = step_x * 9 + step_y * 3
        rows.append(jnp.concatenate([w_sub[first + k] for k in range(3)], 1))
    return jnp.concatenate(rows, 0)


def frame_rows(planes):
    rows = planes.shape[0] * (LY + 2) * LZ
    return jnp.concatenate([planes[:, k : k + LY + 2].reshape(rows, C).astype(BF16) for k in range(3)], 1)


def inner_windows(planes):
    rows = planes.shape[0] * LY * LZ
    return jnp.concatenate([planes[:, k + 1 : k + 1 + LY].reshape(rows, C).astype(BF16) for k in range(3)], 1)


def fold(taps):
    return shift_z(taps[:, :C], 1) + taps[:, C : 2 * C] + shift_z(taps[:, 2 * C :], -1)


def unfold(grad):
    return jnp.concatenate([shift_z(grad, -1), grad, shift_z(grad, 1)], 1).astype(BF16)


def activate(pre_act, hidden_grad):
    sigmoid = 1.0 / (1.0 + jnp.exp(-pre_act))
    pre_grad = hidden_grad * sigmoid * (1.0 + pre_act * (1.0 - sigmoid))
    return pre_act * sigmoid, pre_grad.astype(BF16)


def inner_rows(value):
    return value[:, 1 : LY + 1].reshape(value.shape[0] * LY * LZ, C)


def early_kernel(grid_ref, hidden_ref, y_odd_ref, y_even_ref, w_sub, mid, hidden_mid, pre_ref, taps_ref, inner_ref):
    (low, low_mask, _), (high, high_mask, _) = y_halos(y_odd_ref, y_even_ref)
    mid[:, 0:2] = low.reshape(LX, 2, LZ, C)
    mid[:, LY + 2 :] = high.reshape(LX, 2, LZ, C)
    mid[:, 2 : LY + 2] = grid_ref[...].astype(F32).reshape(LX, LY, LZ, C)
    hidden_mid[:, 0] = low_mask
    hidden_mid[:, LY + 1] = high_mask
    hidden_mid[:, 1 : LY + 1] = hidden_ref[...].astype(F32).reshape(LX, LY, LZ, C)
    rows = frame_rows(mid[...])
    pre_ref[...] = jnp.zeros_like(pre_ref)
    for step_x in range(3):
        part = fold(dot(rows, kernel_rows(w_sub, step_x)))
        pre_ref[2 - step_x : 2 - step_x + LX] += part.reshape(LX, LY + 2, LZ, C)
    inner_ref[...], grad = activate(inner_rows(pre_ref[2:4]), inner_rows(hidden_mid[1:3]))
    spread = unfold(grad.astype(F32))
    for group in range(9):
        step_x, step_y = group // 3, group % 3
        window = mid[step_x : step_x + 2, step_y + 1 : step_y + 1 + LY].reshape(2 * LY * LZ, C)
        taps = dot(window.astype(BF16), spread, ((0,), (0,)))
        for k in range(3):
            taps_ref[(3 * group + k) * C : (3 * group + k + 1) * C] = taps[:, k * C : (k + 1) * C]


def store_half(half, out_ref, mid, side, spread_ref, hidden_ref, place_ref, cot, taps_ref):
    blocks = HALF // C

    def plane(x, step_y):
        source = side[x + 2 if x < 0 else x - 2] if x < 0 or x >= LX else mid[x]
        return source[step_y + 1 : step_y + 1 + LY].reshape(LY * LZ, C)

    for group in range(8) if half == 0 else (7, 8):
        step_x, step_y = group // 3, group % 3
        held = [k for k in range(3) if (3 * group + k) // blocks == half]
        window = jnp.concatenate([plane(step_x - 1, step_y), plane(LX + step_x - 2, step_y)], 0)
        spread = spread_ref[:, held[0] * C : (held[-1] + 1) * C]
        taps = dot(window.astype(BF16), spread, ((0,), (0,)))
        for k in held:
            block = 3 * group + k
            total = taps[:, (k - held[0]) * C : (k - held[0] + 1) * C] + taps_ref[block * C : (block + 1) * C]
            at = (block - half * blocks) * C
            out_ref[at : at + C] = total.astype(BF16)
    if half == 1:
        down = dot(coarse_rows(place_ref, hidden_ref), cot[...], ((0,), (0,))).astype(BF16)
        at = (OFFSETS - blocks) * C
        out_ref[at : at + 8 * C] = down[:, :C]
        out_ref[at + 8 * C : at + 16 * C] = down[:, C:]
        out_ref[at + 16 * C :] = jnp.zeros((HALF - at - 16 * C, C), BF16)


def coarse_rows(place_ref, hidden_ref):
    by_corner = dot(place_ref[...], hidden_ref[...]).astype(BF16)
    return jnp.concatenate([by_corner[k * U_DEV : (k + 1) * U_DEV] for k in range(8)], 1)


def store_of(other, out_ref, *refs):
    held = parity("gx") ^ other
    for half in range(2):
        pl.when(held == half)(functools.partial(store_half, half, out_ref, *refs))


def main_kernel(
    place_ref, ids_ref, mid, hidden_mid, pre_ref, taps_ref, inner_ref, x_odd_ref, x_ends_ref, x_even_ref, cot_ref, w_sub,
    send_ref, spread_ref, hidden_ref, side, side_grad,
):
    x_odd = jnp.concatenate([x_odd_ref[...].astype(F32), x_ends_ref[...].astype(F32)], 0)
    x_even = x_even_ref[...].astype(F32)
    flag = parity("gx")
    side_grad[0] = store_side(side.at[0:2], pick(flag, x_odd, x_even))
    side_grad[1] = store_side(side.at[2:4], pick(flag, x_even, x_odd))
    plane = LY * LZ
    rows = inner_windows(side[1:3])
    first = inner_rows(pre_ref[1:2]) + fold(dot(rows[:plane], kernel_rows(w_sub, 0)))
    last = inner_rows(pre_ref[LX : LX + 1]) + fold(dot(rows[plane:], kernel_rows(w_sub, 2)))
    hidden_grad = [inner_rows(hidden_mid[0:1]), inner_rows(hidden_mid[LX - 1 : LX])]
    outer, grad = activate(jnp.concatenate([first, last], 0), jnp.concatenate(hidden_grad, 0))
    spread_ref[...] = unfold(grad.astype(F32))
    active = dot(cell_onehot(ids_ref[...]), jnp.ones((ids_ref.shape[1], C), BF16)) > 0.5
    hidden = jnp.concatenate([outer[:plane], inner_ref[...], outer[plane:]], 0)
    hidden_ref[...] = jnp.where(active, hidden, 0.0).astype(BF16)
    store_of(1, send_ref, mid, side, spread_ref, hidden_ref, place_ref, cot_ref, taps_ref)


def late_kernel(place_ref, mid, side, spread_ref, hidden_ref, cot_ref, taps_ref, w_down_ref, own_ref, coarse_ref):
    coarse_ref[...] = dot(coarse_rows(place_ref, hidden_ref), w_down_ref[...]).astype(BF16)
    store_of(0, own_ref, mid, side, spread_ref, hidden_ref, place_ref, cot_ref, taps_ref)


def ring_onehot():
    cell = lax.broadcasted_iota(jnp.int32, (12 * LZ, 8 * 32), 0)
    place = lax.broadcasted_iota(jnp.int32, (12 * LZ, 8 * 32), 1)
    z, x, high = cell & 7, (cell >> 3) & 3, (cell >> 5) & 1
    face = ((x & 1) * 4 + (1 - high) * 2 + (z & 1)) * 32 + high * 8 + (x >> 1) * 4 + (z >> 1)
    far, end = (cell >> 4) & 1, (cell >> 3) & 1
    ends = ((1 - far) * 4 + (1 - end) * 2 + (z & 1)) * 32 + 16 + far * 8 + end * 4 + (z >> 1)
    return jnp.where(jnp.where(cell < 8 * LZ, face, ends) == place, 1.0, 0.0).astype(BF16)


def ring_grads(y_odd_ref, y_even_ref, x_ends_ref, x_even_ref, w_down):
    (_, _, low), (_, _, high) = y_halos(y_odd_ref, y_even_ref)

    def tail(ref):
        rows = ref[...].astype(F32)
        rows = rows[rows.shape[0] - 2 * LZ :]
        return jnp.concatenate([rows[:LZ], rows[LZ:]], 1)

    odd, even = tail(x_ends_ref), tail(x_even_ref)
    flag = parity("gx")
    cot = jnp.concatenate([low, high, pick(flag, odd, even), pick(flag, even, odd)], 0).astype(BF16)
    back_rows = dot(cot, w_down[...], ((1,), (1,))).astype(BF16)
    stacked = jnp.concatenate([back_rows[:, k * C : (k + 1) * C] for k in range(8)], 0)
    return dot(ring_onehot(), stacked)


def ring_kernel(
    side, side_grad, hidden_mid, pre_ref, w_sub_ref, y_odd_ref, y_even_ref, x_ends_ref, x_even_ref, w_down, after_ref, grad_ref
):
    column = (LY + 2) * LZ
    centre = kernel_rows(w_sub_ref, 1)
    rows = frame_rows(side[0:2])
    outer = fold(dot(rows, kernel_rows(w_sub_ref, 0)))
    first = pre_ref[0].reshape(column, C) + outer[:column] + fold(dot(rows[column:], centre))
    second = pre_ref[1].reshape(column, C) + outer[column:]
    rows = frame_rows(side[2:4])
    outer = fold(dot(rows, kernel_rows(w_sub_ref, 2)))
    last = pre_ref[LX + 1].reshape(column, C) + outer[column:] + fold(dot(rows[:column], centre))
    before = pre_ref[LX].reshape(column, C) + outer[:column]
    pre_act = jnp.concatenate([first, second, pre_ref[2:LX].reshape(2 * column, C), before, last], 0)
    ring = ring_grads(y_odd_ref, y_even_ref, x_ends_ref, x_even_ref, w_down)
    size = LX * LZ
    faces = [(hidden_mid[:, at] * ring[k * size : (k + 1) * size].reshape(LX, LZ, C))[:, None] for k, at in ((0, 0), (1, LY + 1))]
    middle = jnp.concatenate([faces[0], hidden_mid[:, 1 : LY + 1], faces[1]], 1).reshape(LX * column, C)

    def plane(k):
        first = 2 * size + 2 * LZ * k
        ends = [side_grad[k, :LZ] * ring[first : first + LZ], side_grad[k, column - LZ :] * ring[first + LZ : first + 2 * LZ]]
        return jnp.concatenate([ends[0], side_grad[k, LZ : column - LZ], ends[1]], 0)

    hidden_grad = jnp.concatenate([plane(0), middle, plane(1)], 0)
    _, pre_grad = activate(pre_act, hidden_grad)
    grad_ref[...] = pre_grad


def feature_kernel(ids_ref, grad_ref, w_sub_ref, after_ref, out_ref, done_ref, padded):
    done_ref[...] = jnp.zeros_like(done_ref)
    padded[...] = grad_ref[...].astype(F32).reshape(LX + 2, LY + 2, LZ, C)
    parts = [jnp.zeros((CELLS, C), F32)] * 3
    for step_x in range(3):
        for step_y in range(3):
            window = padded[2 - step_x : 2 - step_x + LX, 2 - step_y : 2 - step_y + LY]
            window = window.reshape(CELLS, C).astype(BF16)
            first = step_x * 9 + step_y * 3
            parts = [parts[k] + dot(window, w_sub_ref[first + k], ((1,), (1,))) for k in range(3)]
    total = shift_z(parts[0], -1) + parts[1] + shift_z(parts[2], 1)
    out_ref[...] = dot(cell_onehot(ids_ref[...]), total.astype(BF16), ((0,), (0,))).astype(BF16)


def add_kernel(own_ref, other_ref, out_ref):
    out_ref[...] = (own_ref[...].astype(F32) + other_ref[...].astype(F32)).astype(BF16)


def sum_kernel(parts_ref, out_ref):
    total = parts_ref[0].astype(F32)
    for k in range(1, PEERS):
        total = total + parts_ref[k].astype(F32)
    out_ref[...] = total.astype(BF16)


def pair_kernel(own_ref, other_ref, *refs):
    out_ref = refs[-1]
    total = (own_ref[...].astype(F32) + other_ref[...].astype(F32)).astype(BF16)
    if len(out_ref.shape) == 2:
        out_ref[...] = total
    else:
        for k in range(PEERS):
            out_ref[k] = total


def unpack_kernel(other, data_ref, *refs):
    sub_hbm, down_hbm, blocks, down, sems = refs[-5:]
    held = parity("gx") ^ other
    first = HALF // C
    rest = OFFSETS - first

    def widen(start, stop):
        rows = data_ref[start * C : stop * C].astype(F32)
        blocks[start:stop] = rows.reshape(stop - start, C, C)

    @pl.when(held == 0)
    def _():
        copies = []
        for k, (start, stop) in enumerate(((0, 6), (6, 12), (12, 17), (17, first))):
            widen(start, stop)
            copies.append(pltpu.make_async_copy(blocks.at[start:stop], sub_hbm.at[start:stop], sems.at[k]))
            copies[-1].start()
        for copy in copies:
            copy.wait()

    @pl.when(held == 1)
    def _():
        widen(0, rest)
        copies = [pltpu.make_async_copy(blocks.at[:rest], sub_hbm.at[first:], sems.at[0])]
        copies[0].start()
        for k, (start, stop) in enumerate(((0, 3), (3, 6), (6, 8))):
            for column in range(2):
                at = (rest + 8 * column + start) * C
                rows = data_ref[at : at + (stop - start) * C].astype(F32)
                down[start * C : stop * C, column * C : (column + 1) * C] = rows
            part = pl.ds(start * C, (stop - start) * C)
            copies.append(pltpu.make_async_copy(down.at[part], down_hbm.at[part], sems.at[k + 1]))
            copies[-1].start()
        for copy in copies:
            copy.wait()


def call(kernel, outs, scratch=(), flops=0, **options):
    return pl.pallas_call(
        kernel,
        out_shape=[jax.ShapeDtypeStruct(*out) for out in outs],
        scratch_shapes=list(scratch),
        cost_estimate=pl.CostEstimate(flops=flops, bytes_accessed=1 << 20, transcendentals=0),
        compiler_params=pltpu.CompilerParams(vmem_limit_bytes=40 * 1024 * 1024),
        **options,
    )


def reduce_all(own, send, first, second):
    rows, cols = lax.axis_size("gx"), lax.axis_size("gy")
    blocks = [
        [i * cols + j for i in range(core, rows, 2) for j in range(first, first + 4)]
        for core in range(2)
        for first in range(0, cols, 4)
    ]

    def trade(value):
        return lax.all_to_all(value, AXES, 0, 0, axis_index_groups=blocks, tiled=True)

    chunk = (CHUNK, C)
    (part,) = call(add_kernel, [((HALF, C), BF16)])(own, swap(send, "gx", 0))
    (total,) = call(sum_kernel, [(chunk, BF16)])(trade(part.reshape(PEERS, *chunk)))
    for flip, shape in ((2, chunk), (6, (PEERS, *chunk))):
        pairs = [(j, ((j >> 1) ^ flip) * 2 + (j & 1)) for j in range(cols)]
        arrived = lax.ppermute(total, "gy", pairs)
        result, mark = first(total) if flip == 2 else second(total, result)
        (total,) = call(pair_kernel, [(shape, BF16)])(total, arrived, mark)
    whole = trade(total).reshape(HALF, C)
    return result, whole, swap(whole, "gx", 0)


def local(features, w_sub, w_down, cell_ids, send_rows, map_in, map_out, cotangent):
    ids = cell_ids[None]
    rows = features.shape[0]
    dense = ((CELLS, C), BF16)
    y_side = ((3 * LX * LZ + 2 * LZ, C), BF16)
    x_face_rows, x_ends = 3 * LY * LZ, 12 * LZ
    packed = ((HALF, C), BF16)
    framed = pltpu.VMEM((LX + 2, LY + 2, LZ, C), F32)

    place = ((CELLS, CELLS), BF16)
    from_corner, to_corner = call(places_kernel, [place, place], flops=LONG)()
    grid, active, y_even, y_odd = call(build_kernel, [dense, dense, y_side, y_side], flops=LONG)(
        from_corner, ids, features, cotangent
    )
    y_even, y_odd = swap_both(y_even, y_odd, "gy")
    hidden_grad, x_odd = call(back_kernel, [dense, ((x_face_rows, C), BF16)], flops=LONG)(
        from_corner, grid, active, cotangent, w_down
    )
    x_odd = swap(x_odd, "gx", 1)
    outs = [((x_face_rows + x_ends, C), BF16), ((x_ends, C), BF16)]
    x_even, x_far = call(x_sides_kernel, outs, flops=LONG)(grid, hidden_grad, y_odd, y_even)
    x_even, x_far = swap_both(x_even, x_far, "gx")
    planes = (LX, LY + 4, LZ, C)
    inner = (2 * LY * LZ, C)
    early = call(
        early_kernel,
        [(planes, F32), ((LX, LY + 2, LZ, C), F32), ((LX + 2, LY + 2, LZ, C), F32), ((OFFSETS * C, C), F32), (inner, F32)],
        flops=LONG,
    )(grid, hidden_grad, y_odd, y_even, w_sub)
    mid, hidden_mid, pre_act, taps, _ = early
    outs = [packed, ((2 * LY * LZ, 3 * C), BF16), dense, (planes, F32), ((2, (LY + 2) * LZ, C), F32)]
    send, spread, hidden, side, side_grad = call(main_kernel, outs, flops=LONG)(
        to_corner, ids, *early, x_odd, x_far, x_even, cotangent, w_sub
    )
    own, coarse = call(late_kernel, [packed, ((U_DEV, C2), BF16)], flops=LONG)(
        to_corner, mid, side, spread, hidden, cotangent, taps, w_down
    )

    def first(value):
        outs = [(((LX + 2) * (LY + 2) * LZ, C), BF16)]
        (grad,) = call(ring_kernel, outs, flops=LONG)(
            side, side_grad, hidden_mid, pre_act, w_sub, y_odd, y_even, x_far, x_even, w_down, value
        )
        return grad, grad

    def second(value, grad):
        outs = [((rows, C), BF16), ((16, C), BF16)]
        return call(feature_kernel, outs, [framed], flops=LONG)(ids, grad, w_sub, value)

    feature_grad, whole, other = reduce_all(own, send, first, second)
    grads = [((OFFSETS, C, C), F32), ((8 * C, C2), F32)]
    scratch = [pltpu.VMEM((HALF // C, C, C), F32), pltpu.VMEM((8 * C, C2), F32), pltpu.SemaphoreType.DMA((4,))]
    in_hbm = [pl.BlockSpec(memory_space=pltpu.HBM)] * 2
    grads_own = call(functools.partial(unpack_kernel, 0), grads, scratch, LONG, out_specs=in_hbm)(whole)
    sub_grad, down_grad = call(
        functools.partial(unpack_kernel, 1),
        grads,
        scratch,
        in_specs=[pl.BlockSpec(memory_space=pltpu.VMEM), *in_hbm],
        out_specs=in_hbm,
        input_output_aliases={1: 0, 2: 1},
    )(other, *grads_own)
    return coarse, feature_grad, sub_grad, down_grad


def solution(mesh):
    rows = P(AXES, None)
    flat = P(AXES)
    maps = P(None, AXES)
    return jax.shard_map(
        local,
        mesh=mesh,
        in_specs=(rows, P(), P(), flat, flat, maps, maps, rows),
        out_specs=(rows, rows, P(), P()),
        check_vma=False,
    )
```

```python
import functools

import jax
import jax.numpy as jnp
from jax import lax
from jax.experimental import pallas as pl
from jax.experimental.pallas import tpu as pltpu
from jax.sharding import PartitionSpec as P

LX = 4
LY = 16
LZ = 8
CELLS = LX * LY * LZ
U_DEV = 64
C = 128
C2 = 256
OFFSETS = 27
AXES = ("gx", "gy")
PEERS = 32
CHUNK = 88
HALF = PEERS * CHUNK
LONG = 1 << 33

F32 = jnp.float32
BF16 = jnp.bfloat16


def swap_pairs(count):
    even = [(k, k ^ 1) for k in range(count)]
    odd = [(k, k + 1 if k % 2 else k - 1) for k in range(count)]
    return even, [(k, m) for k, m in odd if 0 <= m < count]


def swap(value, axis, kind):
    return lax.ppermute(value, axis, swap_pairs(lax.axis_size(axis))[kind])


def swap_both(first, second, axis):
    second = swap(second, axis, 1)
    return swap(first, axis, 0), second


def parity(axis):
    return lax.rem(lax.axis_index(axis), 2)


def pick(flag, when_zero, when_one):
    mask = jnp.full(when_zero.shape, flag, jnp.int32) == 0
    return jnp.where(mask, when_zero, when_one)


def dot(left, right, dims=((1,), (0,))):
    return lax.dot_general(left, right, (dims, ((), ())), preferred_element_type=F32)


def cell_onehot(ids):
    cells = lax.broadcasted_iota(jnp.int32, (CELLS, ids.shape[1]), 0)
    return jnp.where(cells == ids, 1.0, 0.0).astype(BF16)


def corner_onehot(row_axis):
    place = lax.broadcasted_iota(jnp.int32, (CELLS, CELLS), row_axis)
    cell = lax.broadcasted_iota(jnp.int32, (CELLS, CELLS), 1 - row_axis)
    corner, row = place >> 6, place & 63
    x = ((row >> 5) << 1) + (corner >> 2)
    y = (((row >> 2) & 7) << 1) + ((corner >> 1) & 1)
    z = ((row & 3) << 1) + (corner & 1)
    return jnp.where(((x * LY + y) * LZ + z) == cell, 1.0, 0.0).astype(BF16)


def shift_z(value, step):
    rows = value.shape[0]
    z = lax.broadcasted_iota(jnp.int32, value.shape, 0) & (LZ - 1)
    if step == 1:
        return jnp.where(z == 0, 0.0, pltpu.roll(value, 1, 0))
    return jnp.where(z == LZ - 1, 0.0, pltpu.roll(value, rows - 1, 0))


def y_sides(dense, active, cot):
    def face(near, edge):
        first = edge // 2 * (LZ // 2)
        coarse = [cot[k * 32 + first : k * 32 + first + LZ // 2] for k in range(2)]
        coarse = jnp.concatenate(coarse, 0)
        rows = [dense[:, near].reshape(2 * LX * LZ, C), active[:, edge].reshape(LX * LZ, C)]
        return jnp.concatenate([*rows, coarse[:, :C], coarse[:, C:]], 0)

    return face(slice(0, 2), 0), face(slice(LY - 2, LY), LY - 1)


def split_y(rows):
    feature, mask = 2 * LX * LZ, 3 * LX * LZ
    cot = jnp.concatenate([rows[mask : mask + LZ], rows[mask + LZ :]], 1)
    return rows[:feature].reshape(LX, 2 * LZ, C), rows[feature:mask].reshape(LX, LZ, C), cot


def places_kernel(from_ref, to_ref):
    from_ref[...] = corner_onehot(1)
    to_ref[...] = corner_onehot(0)


def place_rows(ids, features):
    onehot = cell_onehot(ids)
    both = dot(onehot, jnp.concatenate([features, jnp.ones(features.shape, BF16)], 1))
    return both[:, :C], both[:, C:]


def build_kernel(place_ref, ids, features, cot, grid_ref, active_ref, even_ref, odd_ref):
    dense, active = place_rows(ids[...], features[...])
    grid_ref[...] = dense.astype(BF16)
    active_ref[...] = active.astype(BF16)
    shape = (LX, LY, LZ, C)
    low, high = y_sides(dense.reshape(shape), active.reshape(shape), cot[...].astype(F32))
    side = parity("gy")
    even_ref[...] = pick(side, high, low).astype(BF16)
    odd_ref[...] = pick(side, low, high).astype(BF16)


def back_kernel(place_ref, grid_ref, active_ref, cot, w_down, hidden_ref, x_odd_ref):
    back_rows = dot(cot[...], w_down[...], ((1,), (1,))).astype(BF16)
    stacked = jnp.concatenate([back_rows[:, k * C : (k + 1) * C] for k in range(8)], 0)
    hidden_grad = jnp.where(active_ref[...].astype(F32) > 0.5, dot(place_ref[...], stacked), 0.0)
    hidden_ref[...] = hidden_grad.astype(BF16)
    dense = grid_ref[...].astype(F32)
    first = x_face(dense, hidden_grad, 0)
    last = x_face(dense, hidden_grad, LX - 1)
    x_odd_ref[...] = pick(parity("gx"), first, last).astype(BF16)


def x_face(dense, hidden_grad, edge):
    plane = LY * LZ
    near = dense[: 2 * plane] if edge == 0 else dense[CELLS - 2 * plane :]
    return jnp.concatenate([near, hidden_grad[edge * plane : (edge + 1) * plane]], 0)


def y_halos(odd_ref, even_ref):
    even, odd = even_ref[...].astype(F32), odd_ref[...].astype(F32)
    side = parity("gy")
    return split_y(pick(side, odd, even)), split_y(pick(side, even, odd))


def x_sides_kernel(grid_ref, hidden_ref, y_odd_ref, y_even_ref, even_ref, odd_ref):
    (low, low_mask, low_cot), (high, high_mask, high_cot) = y_halos(y_odd_ref, y_even_ref)

    def corners(near, edge):
        rows = []
        for x in near:
            rows += [low[x], high[x]]
        at = edge // 2 * (LZ // 2)
        coarse = jnp.concatenate([low_cot[at : at + LZ // 2], high_cot[at : at + LZ // 2]], 0)
        return jnp.concatenate([*rows, low_mask[edge], high_mask[edge], coarse[:, :C], coarse[:, C:]], 0)

    first, last = corners((0, 1), 0), corners((LX - 2, LX - 1), LX - 1)
    dense, hidden_grad = grid_ref[...].astype(F32), hidden_ref[...].astype(F32)
    side = parity("gx")
    face = pick(side, x_face(dense, hidden_grad, LX - 1), x_face(dense, hidden_grad, 0))
    even_ref[...] = jnp.concatenate([face, pick(side, last, first)], 0).astype(BF16)
    odd_ref[...] = pick(side, first, last).astype(BF16)


def store_side(planes, rows):
    face, corner = 2 * LY * LZ, 3 * LY * LZ
    planes[:, 2 : LY + 2] = rows[:face].reshape(2, LY, LZ, C)
    ends = rows[corner : corner + 8 * LZ].reshape(2, 4, LZ, C)
    planes[:, 0:2] = ends[:, 0:2]
    planes[:, LY + 2 :] = ends[:, 2:4]
    grads = corner + 8 * LZ
    return jnp.concatenate([rows[grads : grads + LZ], rows[face:corner], rows[grads + LZ : grads + 2 * LZ]], 0)


def kernel_rows(w_sub, step_x):
    rows = []
    for step_y in range(3):
        first = step_x * 9 + step_y * 3
        rows.append(jnp.concatenate([w_sub[first + k] for k in range(3)], 1))
    return jnp.concatenate(rows, 0)


def frame_rows(planes):
    rows = planes.shape[0] * (LY + 2) * LZ
    return jnp.concatenate([planes[:, k : k + LY + 2].reshape(rows, C).astype(BF16) for k in range(3)], 1)


def inner_windows(planes):
    rows = planes.shape[0] * LY * LZ
    return jnp.concatenate([planes[:, k + 1 : k + 1 + LY].reshape(rows, C).astype(BF16) for k in range(3)], 1)


def fold(taps):
    return shift_z(taps[:, :C], 1) + taps[:, C : 2 * C] + shift_z(taps[:, 2 * C :], -1)


def unfold(grad):
    return jnp.concatenate([shift_z(grad, -1), grad, shift_z(grad, 1)], 1).astype(BF16)


def activate(pre_act, hidden_grad):
    sigmoid = 1.0 / (1.0 + jnp.exp(-pre_act))
    pre_grad = hidden_grad * sigmoid * (1.0 + pre_act * (1.0 - sigmoid))
    return pre_act * sigmoid, pre_grad.astype(BF16)


def inner_rows(value):
    return value[:, 1 : LY + 1].reshape(value.shape[0] * LY * LZ, C)


def early_kernel(grid_ref, hidden_ref, y_odd_ref, y_even_ref, w_sub, mid, hidden_mid, pre_ref, taps_ref, inner_ref):
    (low, low_mask, _), (high, high_mask, _) = y_halos(y_odd_ref, y_even_ref)
    mid[:, 0:2] = low.reshape(LX, 2, LZ, C)
    mid[:, LY + 2 :] = high.reshape(LX, 2, LZ, C)
    mid[:, 2 : LY + 2] = grid_ref[...].astype(F32).reshape(LX, LY, LZ, C)
    hidden_mid[:, 0] = low_mask
    hidden_mid[:, LY + 1] = high_mask
    hidden_mid[:, 1 : LY + 1] = hidden_ref[...].astype(F32).reshape(LX, LY, LZ, C)
    rows = frame_rows(mid[...])
    pre_ref[...] = jnp.zeros_like(pre_ref)
    for step_x in range(3):
        part = fold(dot(rows, kernel_rows(w_sub, step_x)))
        pre_ref[2 - step_x : 2 - step_x + LX] += part.reshape(LX, LY + 2, LZ, C)
    inner_ref[...], grad = activate(inner_rows(pre_ref[2:4]), inner_rows(hidden_mid[1:3]))
    spread = unfold(grad.astype(F32))
    for group in range(9):
        step_x, step_y = group // 3, group % 3
        window = mid[step_x : step_x + 2, step_y + 1 : step_y + 1 + LY].reshape(2 * LY * LZ, C)
        taps = dot(window.astype(BF16), spread, ((0,), (0,)))
        for k in range(3):
            taps_ref[(3 * group + k) * C : (3 * group + k + 1) * C] = taps[:, k * C : (k + 1) * C]


def store_half(half, out_ref, mid, side, spread_ref, hidden_ref, place_ref, cot, taps_ref):
    blocks = HALF // C

    def plane(x, step_y):
        source = side[x + 2 if x < 0 else x - 2] if x < 0 or x >= LX else mid[x]
        return source[step_y + 1 : step_y + 1 + LY].reshape(LY * LZ, C)

    for group in range(8) if half == 0 else (7, 8):
        step_x, step_y = group // 3, group % 3
        held = [k for k in range(3) if (3 * group + k) // blocks == half]
        window = jnp.concatenate([plane(step_x - 1, step_y), plane(LX + step_x - 2, step_y)], 0)
        spread = spread_ref[:, held[0] * C : (held[-1] + 1) * C]
        taps = dot(window.astype(BF16), spread, ((0,), (0,)))
        for k in held:
            block = 3 * group + k
            total = taps[:, (k - held[0]) * C : (k - held[0] + 1) * C] + taps_ref[block * C : (block + 1) * C]
            at = (block - half * blocks) * C
            out_ref[at : at + C] = total.astype(BF16)
    if half == 1:
        down = dot(coarse_rows(place_ref, hidden_ref), cot[...], ((0,), (0,))).astype(BF16)
        at = (OFFSETS - blocks) * C
        out_ref[at : at + 8 * C] = down[:, :C]
        out_ref[at + 8 * C : at + 16 * C] = down[:, C:]
        out_ref[at + 16 * C :] = jnp.zeros((HALF - at - 16 * C, C), BF16)


def coarse_rows(place_ref, hidden_ref):
    by_corner = dot(place_ref[...], hidden_ref[...]).astype(BF16)
    return jnp.concatenate([by_corner[k * U_DEV : (k + 1) * U_DEV] for k in range(8)], 1)


def store_of(other, out_ref, *refs):
    held = parity("gx") ^ other
    for half in range(2):
        pl.when(held == half)(functools.partial(store_half, half, out_ref, *refs))


def main_kernel(
    place_ref, ids_ref, mid, hidden_mid, pre_ref, taps_ref, inner_ref, x_odd_ref, x_ends_ref, x_even_ref, cot_ref, w_sub,
    send_ref, spread_ref, hidden_ref, side, side_grad,
):
    x_odd = jnp.concatenate([x_odd_ref[...].astype(F32), x_ends_ref[...].astype(F32)], 0)
    x_even = x_even_ref[...].astype(F32)
    flag = parity("gx")
    side_grad[0] = store_side(side.at[0:2], pick(flag, x_odd, x_even))
    side_grad[1] = store_side(side.at[2:4], pick(flag, x_even, x_odd))
    plane = LY * LZ
    rows = inner_windows(side[1:3])
    first = inner_rows(pre_ref[1:2]) + fold(dot(rows[:plane], kernel_rows(w_sub, 0)))
    last = inner_rows(pre_ref[LX : LX + 1]) + fold(dot(rows[plane:], kernel_rows(w_sub, 2)))
    hidden_grad = [inner_rows(hidden_mid[0:1]), inner_rows(hidden_mid[LX - 1 : LX])]
    outer, grad = activate(jnp.concatenate([first, last], 0), jnp.concatenate(hidden_grad, 0))
    spread_ref[...] = unfold(grad.astype(F32))
    active = dot(cell_onehot(ids_ref[...]), jnp.ones((ids_ref.shape[1], C), BF16)) > 0.5
    hidden = jnp.concatenate([outer[:plane], inner_ref[...], outer[plane:]], 0)
    hidden_ref[...] = jnp.where(active, hidden, 0.0).astype(BF16)
    store_of(1, send_ref, mid, side, spread_ref, hidden_ref, place_ref, cot_ref, taps_ref)


def late_kernel(place_ref, mid, side, spread_ref, hidden_ref, cot_ref, taps_ref, own_ref):
    store_of(0, own_ref, mid, side, spread_ref, hidden_ref, place_ref, cot_ref, taps_ref)


def ring_onehot():
    cell = lax.broadcasted_iota(jnp.int32, (12 * LZ, 8 * 32), 0)
    place = lax.broadcasted_iota(jnp.int32, (12 * LZ, 8 * 32), 1)
    z, x, high = cell & 7, (cell >> 3) & 3, (cell >> 5) & 1
    face = ((x & 1) * 4 + (1 - high) * 2 + (z & 1)) * 32 + high * 8 + (x >> 1) * 4 + (z >> 1)
    far, end = (cell >> 4) & 1, (cell >> 3) & 1
    ends = ((1 - far) * 4 + (1 - end) * 2 + (z & 1)) * 32 + 16 + far * 8 + end * 4 + (z >> 1)
    return jnp.where(jnp.where(cell < 8 * LZ, face, ends) == place, 1.0, 0.0).astype(BF16)


def ring_grads(y_odd_ref, y_even_ref, x_ends_ref, x_even_ref, w_down):
    (_, _, low), (_, _, high) = y_halos(y_odd_ref, y_even_ref)

    def tail(ref):
        rows = ref[...].astype(F32)
        rows = rows[rows.shape[0] - 2 * LZ :]
        return jnp.concatenate([rows[:LZ], rows[LZ:]], 1)

    odd, even = tail(x_ends_ref), tail(x_even_ref)
    flag = parity("gx")
    cot = jnp.concatenate([low, high, pick(flag, odd, even), pick(flag, even, odd)], 0).astype(BF16)
    back_rows = dot(cot, w_down[...], ((1,), (1,))).astype(BF16)
    stacked = jnp.concatenate([back_rows[:, k * C : (k + 1) * C] for k in range(8)], 0)
    return dot(ring_onehot(), stacked)


def ring_kernel(
    side, side_grad, hidden_mid, pre_ref, w_sub_ref, y_odd_ref, y_even_ref, x_ends_ref, x_even_ref, w_down, place_ref, hidden_ref, after_ref,
    grad_ref, coarse_ref,
):
    coarse_ref[...] = dot(coarse_rows(place_ref, hidden_ref), w_down[...]).astype(BF16)
    column = (LY + 2) * LZ
    centre = kernel_rows(w_sub_ref, 1)
    rows = frame_rows(side[0:2])
    outer = fold(dot(rows, kernel_rows(w_sub_ref, 0)))
    first = pre_ref[0].reshape(column, C) + outer[:column] + fold(dot(rows[column:], centre))
    second = pre_ref[1].reshape(column, C) + outer[column:]
    rows = frame_rows(side[2:4])
    outer = fold(dot(rows, kernel_rows(w_sub_ref, 2)))
    last = pre_ref[LX + 1].reshape(column, C) + outer[column:] + fold(dot(rows[:column], centre))
    before = pre_ref[LX].reshape(column, C) + outer[:column]
    pre_act = jnp.concatenate([first, second, pre_ref[2:LX].reshape(2 * column, C), before, last], 0)
    ring = ring_grads(y_odd_ref, y_even_ref, x_ends_ref, x_even_ref, w_down)
    size = LX * LZ
    faces = [(hidden_mid[:, at] * ring[k * size : (k + 1) * size].reshape(LX, LZ, C))[:, None] for k, at in ((0, 0), (1, LY + 1))]
    middle = jnp.concatenate([faces[0], hidden_mid[:, 1 : LY + 1], faces[1]], 1).reshape(LX * column, C)

    def plane(k):
        first = 2 * size + 2 * LZ * k
        ends = [side_grad[k, :LZ] * ring[first : first + LZ], side_grad[k, column - LZ :] * ring[first + LZ : first + 2 * LZ]]
        return jnp.concatenate([ends[0], side_grad[k, LZ : column - LZ], ends[1]], 0)

    hidden_grad = jnp.concatenate([plane(0), middle, plane(1)], 0)
    _, pre_grad = activate(pre_act, hidden_grad)
    grad_ref[...] = pre_grad


def feature_kernel(ids_ref, grad_ref, w_sub_ref, after_ref, out_ref, done_ref, padded):
    done_ref[...] = jnp.zeros_like(done_ref)
    padded[...] = grad_ref[...].astype(F32).reshape(LX + 2, LY + 2, LZ, C)
    parts = [jnp.zeros((CELLS, C), F32)] * 3
    for step_x in range(3):
        for step_y in range(3):
            window = padded[2 - step_x : 2 - step_x + LX, 2 - step_y : 2 - step_y + LY]
            window = window.reshape(CELLS, C).astype(BF16)
            first = step_x * 9 + step_y * 3
            parts = [parts[k] + dot(window, w_sub_ref[first + k], ((1,), (1,))) for k in range(3)]
    total = shift_z(parts[0], -1) + parts[1] + shift_z(parts[2], 1)
    out_ref[...] = dot(cell_onehot(ids_ref[...]), total.astype(BF16), ((0,), (0,))).astype(BF16)


def add_kernel(own_ref, other_ref, out_ref):
    out_ref[...] = (own_ref[...].astype(F32) + other_ref[...].astype(F32)).astype(BF16)


def sum_kernel(parts_ref, out_ref):
    total = parts_ref[0].astype(F32)
    for k in range(1, PEERS):
        total = total + parts_ref[k].astype(F32)
    out_ref[...] = total.astype(BF16)


def pair_kernel(own_ref, other_ref, *refs):
    out_ref = refs[-1]
    total = (own_ref[...].astype(F32) + other_ref[...].astype(F32)).astype(BF16)
    if len(out_ref.shape) == 2:
        out_ref[...] = total
    else:
        for k in range(PEERS):
            out_ref[k] = total


def unpack_kernel(other, data_ref, *refs):
    sub_hbm, down_hbm, blocks, down, sems = refs[-5:]
    held = parity("gx") ^ other
    first = HALF // C
    rest = OFFSETS - first

    def widen(start, stop):
        rows = data_ref[start * C : stop * C].astype(F32)
        blocks[start:stop] = rows.reshape(stop - start, C, C)

    @pl.when(held == 0)
    def _():
        copies = []
        for k, (start, stop) in enumerate(((0, 6), (6, 12), (12, 17), (17, first))):
            widen(start, stop)
            copies.append(pltpu.make_async_copy(blocks.at[start:stop], sub_hbm.at[start:stop], sems.at[k]))
            copies[-1].start()
        for copy in copies:
            copy.wait()

    @pl.when(held == 1)
    def _():
        widen(0, rest)
        copies = [pltpu.make_async_copy(blocks.at[:rest], sub_hbm.at[first:], sems.at[0])]
        copies[0].start()
        for k, (start, stop) in enumerate(((0, 3), (3, 6), (6, 8))):
            for column in range(2):
                at = (rest + 8 * column + start) * C
                rows = data_ref[at : at + (stop - start) * C].astype(F32)
                down[start * C : stop * C, column * C : (column + 1) * C] = rows
            part = pl.ds(start * C, (stop - start) * C)
            copies.append(pltpu.make_async_copy(down.at[part], down_hbm.at[part], sems.at[k + 1]))
            copies[-1].start()
        for copy in copies:
            copy.wait()


def call(kernel, outs, scratch=(), flops=0, **options):
    return pl.pallas_call(
        kernel,
        out_shape=[jax.ShapeDtypeStruct(*out) for out in outs],
        scratch_shapes=list(scratch),
        cost_estimate=pl.CostEstimate(flops=flops, bytes_accessed=1 << 20, transcendentals=0),
        compiler_params=pltpu.CompilerParams(vmem_limit_bytes=40 * 1024 * 1024),
        **options,
    )


def reduce_all(own, send, first, second):
    rows, cols = lax.axis_size("gx"), lax.axis_size("gy")
    blocks = [
        [i * cols + j for i in range(core, rows, 2) for j in range(first, first + 4)]
        for core in range(2)
        for first in range(0, cols, 4)
    ]

    def trade(value):
        return lax.all_to_all(value, AXES, 0, 0, axis_index_groups=blocks, tiled=True)

    chunk = (CHUNK, C)
    (part,) = call(add_kernel, [((HALF, C), BF16)])(own, swap(send, "gx", 0))
    (total,) = call(sum_kernel, [(chunk, BF16)])(trade(part.reshape(PEERS, *chunk)))
    for flip, shape in ((2, chunk), (6, (PEERS, *chunk))):
        pairs = [(j, ((j >> 1) ^ flip) * 2 + (j & 1)) for j in range(cols)]
        arrived = lax.ppermute(total, "gy", pairs)
        result, mark = first(total) if flip == 2 else second(total, result)
        (total,) = call(pair_kernel, [(shape, BF16)])(total, arrived, mark)
    whole = trade(total).reshape(HALF, C)
    return result, whole, swap(whole, "gx", 0)


def local(features, w_sub, w_down, cell_ids, send_rows, map_in, map_out, cotangent):
    ids = cell_ids[None]
    rows = features.shape[0]
    dense = ((CELLS, C), BF16)
    y_side = ((3 * LX * LZ + 2 * LZ, C), BF16)
    x_face_rows, x_ends = 3 * LY * LZ, 12 * LZ
    packed = ((HALF, C), BF16)
    framed = pltpu.VMEM((LX + 2, LY + 2, LZ, C), F32)

    place = ((CELLS, CELLS), BF16)
    from_corner, to_corner = call(places_kernel, [place, place], flops=LONG)()
    grid, active, y_even, y_odd = call(build_kernel, [dense, dense, y_side, y_side], flops=LONG)(
        from_corner, ids, features, cotangent
    )
    y_even, y_odd = swap_both(y_even, y_odd, "gy")
    hidden_grad, x_odd = call(back_kernel, [dense, ((x_face_rows, C), BF16)], flops=LONG)(
        from_corner, grid, active, cotangent, w_down
    )
    x_odd = swap(x_odd, "gx", 1)
    outs = [((x_face_rows + x_ends, C), BF16), ((x_ends, C), BF16)]
    x_even, x_far = call(x_sides_kernel, outs, flops=LONG)(grid, hidden_grad, y_odd, y_even)
    x_even, x_far = swap_both(x_even, x_far, "gx")
    planes = (LX, LY + 4, LZ, C)
    inner = (2 * LY * LZ, C)
    early = call(
        early_kernel,
        [(planes, F32), ((LX, LY + 2, LZ, C), F32), ((LX + 2, LY + 2, LZ, C), F32), ((OFFSETS * C, C), F32), (inner, F32)],
        flops=LONG,
    )(grid, hidden_grad, y_odd, y_even, w_sub)
    mid, hidden_mid, pre_act, taps, _ = early
    outs = [packed, ((2 * LY * LZ, 3 * C), BF16), dense, (planes, F32), ((2, (LY + 2) * LZ, C), F32)]
    send, spread, hidden, side, side_grad = call(main_kernel, outs, flops=LONG)(
        to_corner, ids, *early, x_odd, x_far, x_even, cotangent, w_sub
    )
    (own,) = call(late_kernel, [packed], flops=LONG)(
        to_corner, mid, side, spread, hidden, cotangent, taps
    )

    def first(value):
        outs = [(((LX + 2) * (LY + 2) * LZ, C), BF16), ((U_DEV, C2), BF16)]
        grad, coarse = call(ring_kernel, outs, flops=LONG)(
            side, side_grad, hidden_mid, pre_act, w_sub, y_odd, y_even, x_far, x_even, w_down, to_corner, hidden, value
        )
        return (grad, coarse), grad

    def second(value, earlier):
        grad, coarse = earlier
        outs = [((rows, C), BF16), ((16, C), BF16)]
        feature_grad, mark = call(feature_kernel, outs, [framed], flops=LONG)(ids, grad, w_sub, value)
        return (feature_grad, coarse), mark

    (feature_grad, coarse), whole, other = reduce_all(own, send, first, second)
    grads = [((OFFSETS, C, C), F32), ((8 * C, C2), F32)]
    scratch = [pltpu.VMEM((HALF // C, C, C), F32), pltpu.VMEM((8 * C, C2), F32), pltpu.SemaphoreType.DMA((4,))]
    in_hbm = [pl.BlockSpec(memory_space=pltpu.HBM)] * 2
    grads_own = call(functools.partial(unpack_kernel, 0), grads, scratch, LONG, out_specs=in_hbm)(whole)
    sub_grad, down_grad = call(
        functools.partial(unpack_kernel, 1),
        grads,
        scratch,
        in_specs=[pl.BlockSpec(memory_space=pltpu.VMEM), *in_hbm],
        out_specs=in_hbm,
        input_output_aliases={1: 0, 2: 1},
    )(other, *grads_own)
    return coarse, feature_grad, sub_grad, down_grad


def solution(mesh):
    rows = P(AXES, None)
    flat = P(AXES)
    maps = P(None, AXES)
    return jax.shard_map(
        local,
        mesh=mesh,
        in_specs=(rows, P(), P(), flat, flat, maps, maps, rows),
        out_specs=(rows, rows, P(), P()),
        check_vma=False,
    )
```
